128 devices in a mesh: row: 4 (over y), gz: 2 (over x_lo), vert: 16 (over z, x_hi, core).
Axes of the slice: x: 4 (x_hi: 2, x_lo: 2; x = x_hi * 2 + x_lo), y: 4, z: 4, core: 2. Of those that a mesh axis runs over, the one named last changes fastest.
Arguments:
- distribution: float32 [32, 32, 110592], P('row', 'gz', 'vert'), may hold values from 0 to 10, as said below
- z_order: int32 [48], P('vert'), may hold values from 0 to 47, as said below
- edge_codes: int32 [2, 4], P(None, 'row'), may hold values from 0 to 2, as said below
Outputs:
- new_distribution: float32 [32, 32, 110592], P('row', 'gz', 'vert')
- macroscopic: float32 [8, 32, 32], P(None, 'row', 'gz')
- boundary_flux: float32 [2, 32], P('gz', 'row')
The draws below stay inside these ranges and needn't reach their ends.
Inputs may be any that keep to these rules, and one draw needn't show every extreme that they name: `z_order`: a permutation of 0 to 47. `edge_codes`: row 0 holds 0 (diffuse wall) or 1 (evaporating film), row 1 holds 0 (diffuse wall) or 2 (outflow); the first column's bottom is film and the last column's top is outflow. `distribution`: every entry is positive.
All inputs are finite; a program needn't handle non-finite values.
Results may differ from the reference program's by a relative error of at most 0.0003.
Values sent between devices are 32-bit elements; how exact they have to be, the bound alone decides.
A program may use at most 128 MiB of HBM per device.

```python
import math
import jax
import jax.numpy as jnp
import numpy as np
from jax import lax

NODES = 8
NVR = 48
NVT = 48
NVZ = 48
STEPS = 2
NER = 4
OUTWARD_COUNT = 32
LENGTHWISE_COUNT = 32
NV = 110592


SPEED_LIMIT = 5.0


def axial_order(key):
    return jax.random.permutation(jax.random.fold_in(key, 11), NVZ).astype(jnp.int32)


def draw_z_order(key, part):
    return axial_order(key)


def draw_edge_codes(key, part):
    bottom = jax.random.randint(jax.random.fold_in(key, 21), (NER,), 0, 2).astype(jnp.int32)
    bottom = bottom.at[0].set(1)
    top_codes = 2 * jax.random.randint(jax.random.fold_in(key, 22), (NER,), 0, 2).astype(jnp.int32)
    top_codes = top_codes.at[NER - 1].set(2)
    return jnp.stack([bottom, top_codes]).astype(jnp.int32)


def uniform_grid(point_count):
    return -SPEED_LIMIT + (jnp.arange(point_count, dtype=jnp.float32) + 0.5) * (2.0 * SPEED_LIMIT / point_count)


def draw_distribution(key, part):
    slot_order = axial_order(key)
    grid_z = uniform_grid(NVZ)
    z_speeds = jnp.sum(jnp.where(slot_order[:, None] == jnp.arange(NVZ)[None, :], grid_z[None, :], 0.0), 1)
    grid_r = uniform_grid(NVR)
    grid_t = uniform_grid(NVT)
    particle_concentration = jnp.exp(jax.random.uniform(jax.random.fold_in(key, 31), (OUTWARD_COUNT, LENGTHWISE_COUNT), jnp.float32, math.log(0.5), math.log(2.0)))
    vapour_warmth = jax.random.uniform(jax.random.fold_in(key, 32), (OUTWARD_COUNT, LENGTHWISE_COUNT), jnp.float32, 0.7, 1.4)
    drift_speed = jax.random.uniform(jax.random.fold_in(key, 33), (3, OUTWARD_COUNT, LENGTHWISE_COUNT), jnp.float32, -0.3, 0.3)
    jitter_scaling = jnp.clip(0.12 * jax.random.normal(jax.random.fold_in(key, 34), (OUTWARD_COUNT, LENGTHWISE_COUNT, NVZ, NVR, NVT), jnp.float32), -0.3, 0.3)
    conduction_strength = jax.random.uniform(jax.random.fold_in(key, 35), (3, OUTWARD_COUNT, LENGTHWISE_COUNT), jnp.float32, 0.15, 0.35)
    conduction_unit_heading = (2 * jax.random.randint(jax.random.fold_in(key, 36), (3, OUTWARD_COUNT, LENGTHWISE_COUNT), 0, 2) - 1).astype(jnp.float32)
    conduction_components = conduction_strength * conduction_unit_heading * (particle_concentration * vapour_warmth ** 1.5)[None]
    fivefold_warmth = vapour_warmth[:, :, None, None, None]
    fivefold_crowding = particle_concentration[:, :, None, None, None]
    pec_z = z_speeds[None, None, :, None, None] - drift_speed[2][:, :, None, None, None]
    pec_r = grid_r[None, None, None, :, None] - drift_speed[0][:, :, None, None, None]
    pec_t = grid_t[None, None, None, None, :] - drift_speed[1][:, :, None, None, None]
    thermal_norm_local = pec_r * pec_r + pec_t * pec_t + pec_z * pec_z
    projected_conduction = pec_r * conduction_components[0][:, :, None, None, None] + pec_t * conduction_components[1][:, :, None, None, None] + pec_z * conduction_components[2][:, :, None, None, None]
    conduction_coefficient = jnp.clip(1.0 + projected_conduction * (thermal_norm_local / fivefold_warmth - 5.0) / (5.0 * fivefold_crowding * fivefold_warmth ** 2), 0.05, 6.0)
    field_entries = fivefold_crowding * fivefold_warmth ** (-1.5) * jnp.exp(-thermal_norm_local / (2 * fivefold_warmth)) * conduction_coefficient * (1.0 + jitter_scaling)
    return field_entries.reshape(OUTWARD_COUNT, LENGTHWISE_COUNT, NVZ * NVR * NVT).astype(jnp.float32)


def setup_inputs(seed: int = 0) -> dict:
    splits = jax.random.split(jax.random.key(seed), 4)
    distribution = draw_distribution(jax.random.fold_in(splits[3], 71), 0)
    z_order = draw_z_order(jax.random.fold_in(splits[3], 71), 0)
    edge_codes = draw_edge_codes(jax.random.fold_in(splits[3], 71), 0)
    return {"distribution": distribution, "z_order": z_order, "edge_codes": edge_codes}


ELEMENT_WIDTH = 4.0
TIME_STEP = 1e-3
KNUDSEN = 0.005
VISCOUS_RATIO = 2.0 / 3.0
SAT_DENSITY = 1.5
SPEED_LIMIT = 5.0
HIGHEST_PRECISION = lax.Precision.HIGHEST


def legendre_pair(position, point_count):
    previous = 1.0
    current = position
    for degree in range(2, point_count + 1):
        previous, current = current, ((2 * degree - 1) * position * current - (degree - 1) * previous) / degree
    slope = point_count * (position * current - previous) / (position * position - 1.0)
    return current, slope


def dg_tables(point_count):
    point_list = []
    weight_list = []
    for number in range(point_count):
        position = math.cos(math.pi * (number + 0.75) / (point_count + 0.5))
        for sweep in range(60):
            value, slope = legendre_pair(position, point_count)
            position = position - value / slope
        value, slope = legendre_pair(position, point_count)
        point_list.append(position)
        weight_list.append(2.0 / ((1.0 - position * position) * slope * slope))
    point_list = point_list[::-1]
    weight_list = weight_list[::-1]
    products = []
    for row_number in range(point_count):
        product_value = 1.0
        for other in range(point_count):
            if other != row_number:
                product_value = product_value * (point_list[row_number] - point_list[other])
        products.append(product_value)
    derivative_rows = []
    for row_number in range(point_count):
        entries = []
        for column in range(point_count):
            if column == row_number:
                total_value = 0.0
                for other in range(point_count):
                    if other != row_number:
                        total_value = total_value + 1.0 / (point_list[row_number] - point_list[other])
                entries.append(total_value)
            else:
                entries.append(products[row_number] / products[column] / (point_list[row_number] - point_list[column]))
        derivative_rows.append(entries)
    right_list = []
    left_list = []
    for column in range(point_count):
        right_value = 1.0
        left_value = 1.0
        for other in range(point_count):
            if other != column:
                right_value = right_value * (1.0 - point_list[other])
                left_value = left_value * (-1.0 - point_list[other])
        right_list.append(right_value / products[column])
        left_list.append(left_value / products[column])
    points = np.array(point_list)
    quad_weights = np.array(weight_list)
    derivative = np.array(derivative_rows)
    end_right = np.array(right_list)
    end_left = np.array(left_list)
    return (points, jnp.asarray(derivative, jnp.float32), jnp.asarray(end_right / quad_weights, jnp.float32),
            jnp.asarray(end_left / quad_weights, jnp.float32), jnp.asarray(end_right, jnp.float32),
            jnp.asarray(end_left, jnp.float32))


def speed_grid(point_count):
    return -SPEED_LIMIT + (np.arange(point_count) + 0.5) * (2.0 * SPEED_LIMIT / point_count)


def velocity_constants():
    weight = (2 * SPEED_LIMIT / NVR) * (2 * SPEED_LIMIT / NVT) * (2 * SPEED_LIMIT / NVZ) / (2 * math.pi) ** 1.5
    grid_r = speed_grid(NVR)
    grid_t = speed_grid(NVT)
    grid_z = speed_grid(NVZ)
    half_flux = weight * np.sum(np.exp(-grid_r ** 2 / 2)) * np.sum(np.exp(-grid_t ** 2 / 2)) * np.sum(
        np.maximum(grid_z, 0.0) * np.exp(-grid_z ** 2 / 2))
    return float(weight), float(half_flux), grid_r, grid_t, grid_z


def shift_velocity(field_entries, offset, keep_mask):
    padding = jnp.zeros(field_entries.shape[:-1] + (abs(offset),), field_entries.dtype)
    if offset > 0:
        shifted = jnp.concatenate([field_entries[..., offset:], padding], -1)
    else:
        shifted = jnp.concatenate([padding, field_entries[..., :offset]], -1)
    return jnp.where(keep_mask, shifted, 0.0)


def rotation_term(field_entries, vel_r, vel_t, radius, a_index, b_index):
    step_r = 2 * SPEED_LIMIT / NVR
    step_t = 2 * SPEED_LIMIT / NVT
    grad_r = (shift_velocity(field_entries, NVT, a_index < NVR - 1) - shift_velocity(field_entries, -NVT, a_index > 0)) / (2 * step_r)
    grad_t = (shift_velocity(field_entries, 1, b_index < NVT - 1) - shift_velocity(field_entries, -1, b_index > 0)) / (2 * step_t)
    return (vel_t * vel_t * grad_r - vel_r * vel_t * grad_t) / radius


def shakhov_term(field_entries, vel_r, vel_t, vel_z, fluid_observables):
    particle_concentration, drift_outward, drift_around, drift_lengthwise, vapour_warmth, conduction_outward, conduction_around, conduction_lengthwise = fluid_observables
    peculiar_r = vel_r - drift_outward
    peculiar_t = vel_t - drift_around
    peculiar_z = vel_z - drift_lengthwise
    thermal_norm_square = peculiar_r ** 2 + peculiar_t ** 2 + peculiar_z ** 2
    projected_conduction = peculiar_r * conduction_outward + peculiar_t * conduction_around + peculiar_z * conduction_lengthwise
    gaussian_resting_state = particle_concentration * vapour_warmth ** -1.5 * jnp.exp(-thermal_norm_square / (2 * vapour_warmth))
    collision_goal_state = gaussian_resting_state * (1.0 + (1.0 - VISCOUS_RATIO) * projected_conduction / (5.0 * particle_concentration * vapour_warmth ** 2) * (thermal_norm_square / vapour_warmth - 5.0))
    return particle_concentration / KNUDSEN * (collision_goal_state - field_entries)


def reference_moments(slabs, z_speeds, vel_r, vel_t, weight, end_right, end_left):
    def first_pass(integral_sums_table, slab_item):
        plane_slab, z_speed = slab_item
        bottom = jnp.einsum('j,rjp->rp', end_left, plane_slab[:, :NODES], precision=HIGHEST_PRECISION)
        top_trace = jnp.einsum('j,rjp->rp', end_right, plane_slab[:, LENGTHWISE_COUNT - NODES:], precision=HIGHEST_PRECISION)
        speed_sq = vel_r ** 2 + vel_t ** 2 + z_speed ** 2
        plain = jnp.sum(plane_slab, -1)
        return (integral_sums_table[0] + weight * plain,
                integral_sums_table[1] + weight * jnp.sum(plane_slab * vel_r, -1),
                integral_sums_table[2] + weight * jnp.sum(plane_slab * vel_t, -1),
                integral_sums_table[3] + weight * z_speed * plain,
                integral_sums_table[4] + 0.5 * weight * jnp.sum(plane_slab * speed_sq, -1),
                integral_sums_table[5] + weight * jnp.maximum(-z_speed, 0.0) * jnp.sum(bottom, -1),
                integral_sums_table[6] + weight * jnp.maximum(z_speed, 0.0) * jnp.sum(top_trace, -1),
                integral_sums_table[7] + weight * jnp.maximum(-z_speed, 0.0) * jnp.sum(top_trace, -1)), None

    node_zeros = jnp.zeros((OUTWARD_COUNT, LENGTHWISE_COUNT), jnp.float32)
    edge_zeros = jnp.zeros((OUTWARD_COUNT,), jnp.float32)
    start = (node_zeros,) * 5 + (edge_zeros,) * 3
    integral_sums_table, _ = lax.scan(first_pass, start, (slabs, z_speeds))
    particle_concentration = integral_sums_table[0]
    drift_outward = integral_sums_table[1] / particle_concentration
    drift_around = integral_sums_table[2] / particle_concentration
    drift_lengthwise = integral_sums_table[3] / particle_concentration
    vapour_warmth = (2.0 * integral_sums_table[4] / particle_concentration - (drift_outward ** 2 + drift_around ** 2 + drift_lengthwise ** 2)) / 3.0

    def second_pass(heat_totals, slab_item):
        plane_slab, z_speed = slab_item
        peculiar_r = vel_r - drift_outward[:, :, None]
        peculiar_t = vel_t - drift_around[:, :, None]
        peculiar_z = z_speed - drift_lengthwise[:, :, None]
        weighted = plane_slab * (peculiar_r ** 2 + peculiar_t ** 2 + peculiar_z ** 2)
        return (heat_totals[0] + 0.5 * weight * jnp.sum(weighted * peculiar_r, -1),
                heat_totals[1] + 0.5 * weight * jnp.sum(weighted * peculiar_t, -1),
                heat_totals[2] + 0.5 * weight * jnp.sum(weighted * peculiar_z, -1)), None

    conduction_integral, _ = lax.scan(second_pass, (node_zeros,) * 3, (slabs, z_speeds))
    fluid_observables = (particle_concentration, drift_outward, drift_around, drift_lengthwise, vapour_warmth, conduction_integral[0], conduction_integral[1], conduction_integral[2])
    return fluid_observables, (integral_sums_table[5], integral_sums_table[6], integral_sums_table[7])


def reference(distribution, z_order, edge_codes):
    points, derivative, lift_right, lift_left, end_right, end_left = dg_tables(NODES)
    weight, half_flux, grid_r, grid_t, grid_z = velocity_constants()
    plane_size = NVR * NVT
    vel_r = jnp.asarray(np.repeat(grid_r, NVT), jnp.float32)
    vel_t = jnp.asarray(np.tile(grid_t, NVR), jnp.float32)
    plane_index = jnp.arange(plane_size, dtype=jnp.int32)
    a_index = plane_index // NVT
    b_index = plane_index % NVT
    z_speeds = jnp.asarray(grid_z, jnp.float32)[z_order]
    elements = OUTWARD_COUNT // NODES
    columns = LENGTHWISE_COUNT // NODES
    radius = ((jnp.arange(elements, dtype=jnp.float32)[:, None] + (1.0 + jnp.asarray(points, jnp.float32))[None, :] / 2)
              * ELEMENT_WIDTH).reshape(OUTWARD_COUNT)
    code_bottom = jnp.repeat(edge_codes[0], NODES)
    code_top = jnp.repeat(edge_codes[1], NODES)
    slabs = distribution.reshape(OUTWARD_COUNT, LENGTHWISE_COUNT, NVZ, plane_size).transpose(2, 0, 1, 3)

    for step_index in range(STEPS):
        fluid_observables, edge_sums = reference_moments(slabs, z_speeds, vel_r, vel_t, weight, end_right, end_left)
        bottom_density = jnp.where(code_bottom == 1, SAT_DENSITY, edge_sums[0] / half_flux)
        top_density = edge_sums[1] / half_flux
        node_stats = tuple(entry[:, :, None] for entry in fluid_observables)

        def advance_slab(slab_item):
            plane_slab, z_speed = slab_item
            maxwell_wall = jnp.exp(-(vel_r ** 2 + vel_t ** 2 + z_speed ** 2) / 2)
            grouped = plane_slab.reshape(elements, NODES, LENGTHWISE_COUNT, plane_size)
            volume = jnp.einsum('ij,ejzp->eizp', derivative, grouped, precision=HIGHEST_PRECISION)
            trace_hi = jnp.einsum('j,ejzp->ezp', end_right, grouped, precision=HIGHEST_PRECISION)
            trace_lo = jnp.einsum('j,ejzp->ezp', end_left, grouped, precision=HIGHEST_PRECISION)
            mirror = trace_lo[0].reshape(LENGTHWISE_COUNT, NVR, NVT)[:, ::-1, :].reshape(LENGTHWISE_COUNT, plane_size)
            plus_side = jnp.concatenate([mirror[None], trace_hi], 0)
            minus_side = jnp.concatenate([trace_lo, trace_hi[-1:]], 0)
            face_values = jnp.where(vel_r > 0, plus_side, minus_side)
            radial = (2.0 / ELEMENT_WIDTH) * vel_r * (volume
                                                      + lift_right[None, :, None, None] * (face_values[1:] - trace_hi)[:, None]
                                                      - lift_left[None, :, None, None] * (face_values[:-1] - trace_lo)[:, None])
            radial = radial.reshape(OUTWARD_COUNT, LENGTHWISE_COUNT, plane_size)
            grouped = plane_slab.reshape(OUTWARD_COUNT, columns, NODES, plane_size)
            volume = jnp.einsum('ij,rejp->reip', derivative, grouped, precision=HIGHEST_PRECISION)
            trace_hi = jnp.einsum('j,rejp->rep', end_right, grouped, precision=HIGHEST_PRECISION)
            trace_lo = jnp.einsum('j,rejp->rep', end_left, grouped, precision=HIGHEST_PRECISION)
            bottom_ghost = bottom_density[:, None] * maxwell_wall
            top_ghost = jnp.where(code_top[:, None] == 2, trace_hi[:, -1], top_density[:, None] * maxwell_wall)
            plus_side = jnp.concatenate([bottom_ghost[:, None], trace_hi], 1)
            minus_side = jnp.concatenate([trace_lo, top_ghost[:, None]], 1)
            face_values = jnp.where(z_speed > 0, plus_side, minus_side)
            axial_term = (2.0 / ELEMENT_WIDTH) * z_speed * (volume
                                                            + lift_right[None, None, :, None] * (face_values[:, 1:] - trace_hi)[:, :, None]
                                                            - lift_left[None, None, :, None] * (face_values[:, :-1] - trace_lo)[:, :, None])
            axial_term = axial_term.reshape(OUTWARD_COUNT, LENGTHWISE_COUNT, plane_size)
            rotation = rotation_term(plane_slab, vel_r, vel_t, radius[:, None, None], a_index, b_index)
            collide = shakhov_term(plane_slab, vel_r, vel_t, z_speed, node_stats)
            return plane_slab + TIME_STEP * (collide - radial - axial_term - rotation)

        slabs = lax.map(advance_slab, (slabs, z_speeds))

    fluid_observables, edge_sums = reference_moments(slabs, z_speeds, vel_r, vel_t, weight, end_right, end_left)
    macroscopic = jnp.stack(fluid_observables)
    bottom_row = jnp.where(code_bottom == 1, SAT_DENSITY * half_flux - edge_sums[0], 0.0)
    top_row = jnp.where(code_top == 2, edge_sums[1] - edge_sums[2], 0.0)
    boundary_flux = jnp.stack([bottom_row, top_row])
    new_distribution = slabs.transpose(1, 2, 0, 3).reshape(OUTWARD_COUNT, LENGTHWISE_COUNT, NV)
    return new_distribution, macroscopic, boundary_flux
```

```python
import functools
import math

import jax
import jax.numpy as jnp
import ml_dtypes
import numpy as np
from jax import lax
from jax.experimental import pallas as pl
from jax.experimental.pallas import tpu as pltpu
from jax.sharding import PartitionSpec as P

NODES = 8
NVR = 48
NVT = 48
NVZ = 48
STEPS = 2

ELEMENT_WIDTH = 4.0
TIME_STEP = 0.001
KNUDSEN = 0.005
VISCOUS_RATIO = 2.0 / 3.0
SAT_DENSITY = 1.5
SPEED_LIMIT = 5.0

PLANE = NVR * NVT
HALF = PLANE // 2
GRID_STEP = 2 * SPEED_LIMIT / NVR
UNIT = GRID_STEP / 2
MESH_IDS = pl.DeviceIdType.MESH
F32 = jnp.float32
BF16 = jnp.bfloat16


def legendre_pair(position, point_count):
    previous = 1.0
    current = position
    for degree in range(2, point_count + 1):
        previous, current = (
            current,
            ((2 * degree - 1) * position * current - (degree - 1) * previous) / degree,
        )
    slope = point_count * (position * current - previous) / (position * position - 1.0)
    return (current, slope)


def dg_tables(point_count):
    point_list = []
    weight_list = []
    for number in range(point_count):
        position = math.cos(math.pi * (number + 0.75) / (point_count + 0.5))
        for sweep in range(60):
            value, slope = legendre_pair(position, point_count)
            position = position - value / slope
        value, slope = legendre_pair(position, point_count)
        point_list.append(position)
        weight_list.append(2.0 / ((1.0 - position * position) * slope * slope))
    point_list = point_list[::-1]
    weight_list = weight_list[::-1]
    products = []
    for row_number in range(point_count):
        product_value = 1.0
        for other in range(point_count):
            if other != row_number:
                product_value = product_value * (point_list[row_number] - point_list[other])
        products.append(product_value)
    derivative_rows = []
    for row_number in range(point_count):
        entries = []
        for column in range(point_count):
            if column == row_number:
                total_value = 0.0
                for other in range(point_count):
                    if other != row_number:
                        total_value = total_value + 1.0 / (
                            point_list[row_number] - point_list[other]
                        )
                entries.append(total_value)
            else:
                entries.append(
                    products[row_number]
                    / products[column]
                    / (point_list[row_number] - point_list[column])
                )
        derivative_rows.append(entries)
    right_list = []
    left_list = []
    for column in range(point_count):
        right_value = 1.0
        left_value = 1.0
        for other in range(point_count):
            if other != column:
                right_value = right_value * (1.0 - point_list[other])
                left_value = left_value * (-1.0 - point_list[other])
        right_list.append(right_value / products[column])
        left_list.append(left_value / products[column])
    points = np.array(point_list)
    quad_weights = np.array(weight_list)
    derivative = np.array(derivative_rows)
    end_right = np.array(right_list)
    end_left = np.array(left_list)
    return (
        points,
        derivative,
        end_right / quad_weights,
        end_left / quad_weights,
        end_right,
        end_left,
    )


def speed_grid(point_count):
    return -SPEED_LIMIT + (np.arange(point_count) + 0.5) * (2.0 * SPEED_LIMIT / point_count)


def split_exact(values, count):
    parts = []
    rest = np.asarray(values, np.float64)
    for _ in range(count):
        head = rest.astype(ml_dtypes.bfloat16).astype(np.float64)
        parts.append(head)
        rest = rest - head
    assert not np.any(rest)
    return parts


def constants():
    points, derivative, lift_right, lift_left, end_right, end_left = dg_tables(NODES)
    eye8, eye16 = np.eye(8), np.eye(16)
    scale = -TIME_STEP * 2.0 / ELEMENT_WIDTH
    plus = derivative + np.outer(lift_left, end_left)
    minus = derivative - np.outer(lift_right, end_right)
    radial = np.zeros((3, 128, 160))
    for k, (core, ghost) in enumerate(
        [(minus, lift_right), (derivative, 0 * lift_right), (plus, -lift_left)]
    ):
        radial[k, :, :128] = np.kron(core, eye16)
        radial[k, :, 128:144] = np.kron(ghost[:, None], eye16)
    up = np.zeros((16, 16))
    up[:8, :8] = plus
    up[8:, 8:] = plus
    up[8:, :8] = -np.outer(lift_left, end_right)
    down = np.zeros((16, 16))
    down[:8, :8] = minus
    down[8:, 8:] = minus
    down[:8, 8:] = np.outer(lift_right, end_left)
    outflow = down.copy()
    outflow[8:, 8:] = derivative
    none = np.zeros(16)
    up_ghost = np.concatenate([-lift_left, np.zeros(8)])
    down_ghost = np.concatenate([np.zeros(8), lift_right])
    axial = np.zeros((5, 128, 160))
    for k, (core, ghost) in enumerate(
        [(up, none), (up, up_ghost), (down, down_ghost), (down, none), (outflow, none)]
    ):
        axial[k, :, :128] = np.kron(eye8, core)
        axial[k, :, 144:152] = np.kron(eye8, ghost[:, None])
    low_first = np.concatenate([end_left, np.zeros(8)])
    high_last = np.concatenate([np.zeros(8), end_right])
    trace = np.zeros((2, 2, 32, 128))
    for g, across in enumerate([high_last, low_first]):
        for h, along in enumerate([end_left, end_right]):
            trace[g, h, :16] = np.kron(along[None, :], eye16)
            trace[g, h, 16:24] = np.kron(eye8, across[None, :])
    odd = 2.0 * np.arange(48) + 1 - 48
    nr, nt = np.repeat(odd, 48), np.tile(odd, 48)
    square = nr * nr + nt * nt
    columns = (
        [np.ones(PLANE), nr, nt]
        + split_exact(nr * nr, 2)
        + split_exact(nt * nt, 2)
        + split_exact(nr * nt, 2)
        + split_exact(nr * square, 3)
        + split_exact(nt * square, 3)
        + [np.zeros(PLANE)]
    )
    basis = np.stack(columns)
    grid = speed_grid(48)
    vr, vt = np.repeat(grid, 48), np.tile(grid, 48)
    a, b = np.repeat(np.arange(48), 48), np.tile(np.arange(48), 48)
    turn_r = -TIME_STEP * vt * vt / (2 * GRID_STEP)
    turn_t = TIME_STEP * vr * vt / (2 * GRID_STEP)
    rows = np.stack(
        [
            vr,
            vt,
            np.exp(-(vr**2 + vt**2) / 2),
            turn_r * (a < 47),
            -turn_r * (a > 0),
            turn_t * (b < 47),
            -turn_t * (b > 0),
            0 * vr,
        ]
    )
    ones8 = np.ones(8)
    edge = np.zeros((128, 384))
    edge[:, :128] = np.kron(eye8, np.outer(low_first, np.ones(16)))
    edge[:, 128:256] = np.kron(eye8, np.outer(high_last, np.ones(16)))
    edge[:, 256:264] = np.kron(eye8, low_first[:, None])
    edge[:, 264:272] = np.kron(eye8, high_last[:, None])
    wall = np.zeros((8, 128))
    wall[0] = np.kron(ones8, np.concatenate([-scale * lift_left, np.zeros(8)]))
    wall[1] = np.kron(ones8, np.concatenate([np.zeros(8), scale * lift_right]))
    weight = GRID_STEP**3 / (2 * math.pi) ** 1.5
    half_flux = (
        weight
        * np.sum(np.exp(-(grid**2) / 2)) ** 2
        * np.sum(np.maximum(grid, 0.0) * np.exp(-(grid**2) / 2))
    )
    as_bf16 = lambda x: jnp.asarray(x.astype(np.float32).astype(ml_dtypes.bfloat16))
    as_f32 = lambda x: jnp.asarray(x.astype(np.float32))
    arrays = (
        as_bf16(scale * radial),
        as_f32(scale * axial),
        as_bf16(trace),
        as_bf16(basis),
        as_f32(rows),
        as_f32(edge),
        as_f32(wall),
    )
    return arrays, float(weight), float(half_flux), [float(x) for x in points]


def kernel(
    sizes, weight, half_flux, points,
    f_hbm, order, codes, radial_hbm, axial_hbm, trace_hbm, basis_hbm, rows_hbm, edge_hbm, wall_hbm,
    out_hbm, macro, flux,
    F, X, LO, PART, TOUT, LHS, EX, PP, SM, PR, PT,
    radial, axial, trace, basis, rows, edge, wall,
    trR, trA, ghR, ghA, mine, ARB,
    load_sem, const_sem, out_sem,
    rs_send, rs_recv, as_send, as_recv, ar_send, ar_recv,
):
    row_total, vert_total = sizes
    row, gz, vert = lax.axis_index("row"), lax.axis_index("gz"), lax.axis_index("vert")
    last_row = row_total - 1

    barrier = pltpu.get_barrier_semaphore()

    def hello(k, carry):
        peer = lax.rem(vert + k, vert_total)
        pl.semaphore_signal(barrier, inc=1, device_id=(row, gz, peer), device_id_type=MESH_IDS)
        return carry

    lax.fori_loop(1, vert_total, hello, 0)
    pl.semaphore_signal(barrier, inc=1, device_id=(row, 1 - gz, vert), device_id_type=MESH_IDS)

    @pl.when(row > 0)
    def _():
        pl.semaphore_signal(barrier, inc=1, device_id=(row - 1, gz, vert), device_id_type=MESH_IDS)

    @pl.when(row < last_row)
    def _():
        pl.semaphore_signal(barrier, inc=1, device_id=(row + 1, gz, vert), device_id_type=MESH_IDS)

    loads = [
        pltpu.make_async_copy(f_hbm.at[:, pl.ds(s * PLANE, PLANE)], F.at[s], load_sem.at[s])
        for s in range(3)
    ]
    consts = [
        pltpu.make_async_copy(src, dst, const_sem.at[k])
        for k, (src, dst) in enumerate(
            [
                (trace_hbm, trace),
                (basis_hbm, basis),
                (rows_hbm, rows),
                (radial_hbm, radial),
                (axial_hbm, axial),
                (edge_hbm, edge),
                (wall_hbm, wall),
            ]
        )
    ]
    loads[0].start()
    for copy in consts[:2]:
        copy.start()
    for copy in loads[1:]:
        copy.start()
    for copy in consts[2:]:
        copy.start()

    speeds = [(2 * order[s] - (NVZ - 1)).astype(F32) * UNIT for s in range(3)]
    bottom_code, top_code = codes[0, 0], codes[1, 0]
    zero16 = jnp.zeros((16, HALF), F32)

    def radial_copy(n, s, h):
        step = 1 if h else -1
        return pltpu.make_async_remote_copy(
            src_ref=trR.at[n, s, h],
            dst_ref=ghR.at[n, s, h],
            send_sem=rs_send.at[n, s, h],
            recv_sem=rs_recv.at[n, s, h],
            device_id=(row + step, gz, vert),
            device_id_type=MESH_IDS,
        )

    def axial_copy(n, s):
        return pltpu.make_async_remote_copy(
            src_ref=trA.at[n, s],
            dst_ref=ghA.at[n, s],
            send_sem=as_send.at[n, s],
            recv_sem=as_recv.at[n, s],
            device_id=(row, 1 - gz, vert),
            device_id_type=MESH_IDS,
        )

    def sum_copy(n, slot, peer, k):
        return pltpu.make_async_remote_copy(
            src_ref=mine.at[n],
            dst_ref=ARB.at[n, slot],
            send_sem=ar_send.at[n, k],
            recv_sem=ar_recv.at[n, slot],
            device_id=(row, gz, peer),
            device_id_type=MESH_IDS,
        )

    def send_halo(n, s):
        @pl.when(row > 0)
        def _():
            radial_copy(n, s, 0).start()

        @pl.when(row < last_row)
        def _():
            radial_copy(n, s, 1).start()

        axial_copy(n, s).start()

    def traces(n, s):
        for h in range(2):
            lanes = pl.ds(h * HALF, HALF)
            both = jnp.dot(trace[gz, h], X[s, 0:128, lanes], preferred_element_type=F32)
            trR[n, s, h] = both[0:16]
            trA[n, s, :, lanes] = both[16:24]

    def missing_ghosts(n, s):
        @pl.when(row == 0)
        def _():
            low = trR[n, s, 0]
            ghR[n, s, 1] = jnp.concatenate(
                [low[:, k * NVT : (k + 1) * NVT] for k in reversed(range(NVR // 2))], axis=1
            )

        @pl.when(row == last_row)
        def _():
            ghR[n, s, 0] = zero16

    def plane_sums(s):
        dims = (((1,), (1,)), ((), ()))
        table = lax.dot_general(basis[...], X[s, 0:128], dims, preferred_element_type=F32)
        table += lax.dot_general(basis[...], LO[s], dims, preferred_element_type=F32)
        z = speeds[s]
        g = [table[i : i + 1] for i in range(15)]
        b0, br, bt = g[0], UNIT * g[1], UNIT * g[2]
        brr, btt, brt = (UNIT**2 * (g[i] + g[i + 1]) for i in (3, 5, 7))
        br3, bt3 = (UNIT**3 * (g[i] + (g[i + 1] + g[i + 2])) for i in (9, 12))
        return [
            b0,
            br,
            bt,
            jnp.maximum(z, 0.0) * b0,
            jnp.maximum(-z, 0.0) * b0,
            brr,
            btt,
            z * z * b0,
            brt,
            z * br,
            z * bt,
            br3 + z * z * br,
            bt3 + z * z * bt,
            z * (brr + btt) + (z * z * z) * b0,
        ]

    def send_sums(n, parts):
        total = [parts[0][i] + (parts[1][i] + parts[2][i]) for i in range(14)]
        for i in range(14):
            mine[n, i : i + 1] = total[i]
        mine[n, 14:16] = jnp.zeros((2, 128), F32)
        ARB[n, vert] = mine[n]

        def send(k, carry):
            sum_copy(n, vert, lax.rem(vert + k, vert_total), k).start()
            return carry

        lax.fori_loop(1, vert_total, send, 0)

    def wait_sums(n):
        def wait(k, carry):
            source = lax.rem(vert + k, vert_total)
            sum_copy(n, source, source, k).wait_recv()
            return carry

        lax.fori_loop(1, vert_total, wait, 0)
        terms = [ARB[n, k] for k in range(vert_total)]
        while len(terms) > 1:
            terms = [terms[i] + terms[i + 1] for i in range(0, len(terms), 2)]
        return terms[0]

    def observables(S):
        m = [S[i : i + 1] for i in range(14)]
        inv = 1.0 / m[0]
        u = [m[1] * inv, m[2] * inv, (m[3] - m[4]) * inv]
        usq = u[0] * u[0] + u[1] * u[1] + u[2] * u[2]
        tr = m[5] + m[6] + m[7]
        temp = (tr * inv - usq) / 3.0
        tensor = [[m[5], m[8], m[9]], [m[8], m[6], m[10]], [m[9], m[10], m[7]]]
        heat = []
        for i in range(3):
            mixed = tensor[i][0] * u[0] + tensor[i][1] * u[1] + tensor[i][2] * u[2]
            raw = m[11 + i] - 2.0 * mixed - u[i] * tr + (2.0 * usq * m[0]) * u[i]
            heat.append((0.5 * weight) * raw)
        return weight * m[0], u, temp, heat

    def params(S):
        density, u, temp, heat = observables(S)
        edges = jnp.dot(S, edge[:, 0:256], preferred_element_type=F32, precision=lax.Precision.HIGHEST)
        incident = weight * edges[4:5, 0:128]
        upward = weight * edges[3:4, 128:256]
        bottom = jnp.where(bottom_code == 1, SAT_DENSITY, incident / half_flux)
        top = jnp.where(top_code == 2, 0.0, upward / half_flux)
        wall_gain = jnp.where(gz == 0, bottom * wall[0:1], top * wall[1:2])
        inv_temp = 1.0 / temp
        kappa = ((1.0 - VISCOUS_RATIO) / 5.0) * inv_temp * inv_temp / density
        rate = (TIME_STEP / KNUDSEN) * density
        peak = rate * density * inv_temp * lax.rsqrt(temp)
        out = [u[0], u[1], inv_temp, kappa * heat[0], kappa * heat[1], 1.0 - rate]
        for s in range(3):
            z = speeds[s]
            cz = z - u[2]
            inward = jnp.where(gz == 0, jnp.maximum(z, 0.0), jnp.minimum(z, 0.0))
            out += [
                kappa * heat[2] * cz,
                cz * cz * inv_temp,
                peak * jnp.exp(-0.5 * cz * cz * inv_temp),
                inward * wall_gain * jnp.exp(jnp.zeros((1, 128), F32) - 0.5 * z * z),
            ]
        for i, value in enumerate(out):
            PR[i : i + 1] = value
        PT[...] = PR[...].T

    PR[...] = jnp.zeros((128, 128), F32)
    for copy in consts[:2]:
        copy.wait()
    parts = []
    for s in range(3):
        loads[s].wait()

        def split(r, carry, s=s):
            at = pl.ds(pl.multiple_of(r * 16, 16), 16)
            x = F[s, at, :]
            hi = x.astype(BF16)
            X[s, at, :] = hi
            LO[s, at, :] = (x - hi.astype(F32)).astype(BF16)
            return carry

        lax.fori_loop(0, 8, split, 0)
        traces(0, s)
        if s == 0:
            peers = vert_total + (row > 0).astype(jnp.int32) + (row < last_row).astype(jnp.int32)
            pl.semaphore_wait(barrier, peers)

        send_halo(0, s)
        parts.append(plane_sums(s))
    send_sums(0, parts)

    for copy in consts[2:]:
        copy.wait()
    for s in range(3):
        z = speeds[s]
        up = jnp.where(gz == 0, axial[0], axial[1])
        down = jnp.where(gz == 0, axial[2], jnp.where(top_code == 2, axial[4], axial[3]))
        along = (z * jnp.where(z > 0, up, down)).astype(BF16)
        for h in range(2):
            LHS[s, h, 128:256] = along
        LHS[s, 0, 0:128] = radial[jnp.where(row == last_row, 1, 0)]
        LHS[s, 1, 0:128] = radial[2]

    first = row.astype(F32)

    for n in range(STEPS):
        def rotate(r, carry):
            at = pl.ds(pl.multiple_of(r * 16, 16), 16)
            place = 0.0
            for i in range(NODES):
                place = jnp.where(r == i, (1.0 + points[i]) / 2, place)
            scale = 1.0 / ((first + place) * ELEMENT_WIDTH + jnp.zeros((16, 128), F32))
            scale = scale[:, 0:1]
            for s in range(3):
                x = F[s, at, :]
                turn = (
                    rows[3:4] * pltpu.roll(x, PLANE - NVT, 1)
                    + rows[4:5] * pltpu.roll(x, NVT, 1)
                    + rows[5:6] * pltpu.roll(x, PLANE - 1, 1)
                    + rows[6:7] * pltpu.roll(x, 1, 1)
                )
                PART[s, at, :] = turn * scale
            return carry

        lax.fori_loop(0, 8, rotate, 0)

        for s in range(3):
            missing_ghosts(n, s)

            @pl.when(row < last_row)
            def _():
                radial_copy(n, s, 0).wait_recv()

            @pl.when(row > 0)
            def _():
                radial_copy(n, s, 1).wait_recv()

            axial_copy(n, s).wait_recv()
            X[s, 144:160, :] = jnp.concatenate(
                [ghA[n, s], jnp.zeros((8, PLANE), F32)], axis=0
            ).astype(BF16)
            for h in range(2):
                lanes = pl.ds(h * HALF, HALF)
                X[s, 128:144, lanes] = ghR[n, s, h].astype(BF16)
                TOUT[s, :, lanes] = jnp.dot(
                    LHS[s, h], X[s, :, lanes], preferred_element_type=F32
                )

        params(wait_sums(n))

        def plane(r, carry):
            at = pl.ds(pl.multiple_of(r * 16, 16), 16)
            cr = rows[0:1] - PT[at, 0:1]
            ct = rows[1:2] - PT[at, 1:2]
            inv_temp = PT[at, 2:3]
            square = cr * cr + ct * ct
            EX[at, :] = jnp.exp(square * (-0.5 * inv_temp))
            SM[at, :] = square * inv_temp - 5.0
            PP[at, :] = cr * PT[at, 3:4] + ct * PT[at, 4:5]
            return carry

        lax.fori_loop(0, 8, plane, 0)

        parts = []
        for s in range(3):

            def update(r, carry, s=s):
                at = pl.ds(pl.multiple_of(r * 16, 16), 16)
                below = pl.ds(pl.multiple_of(r * 16 + 128, 16), 16)
                keep = PT[at, 5:6]
                a_s, b_s, c_s, w_s = (PT[at, 6 + 4 * s + i : 7 + 4 * s + i] for i in range(4))
                for j in range(6):
                    lanes = pl.ds(j * 384, 384)
                    goal = (EX[at, lanes] * c_s) * (
                        1.0 + (PP[at, lanes] + a_s) * (SM[at, lanes] + b_s)
                    )
                    x = (
                        keep * F[s, at, lanes]
                        + PART[s, at, lanes]
                        + rows[0:1, lanes] * TOUT[s, at, lanes]
                        + TOUT[s, below, lanes]
                        + w_s * rows[2:3, lanes]
                        + goal
                    )
                    F[s, at, lanes] = x
                    hi = x.astype(BF16)
                    X[s, at, lanes] = hi
                    LO[s, at, lanes] = (x - hi.astype(F32)).astype(BF16)
                return carry

            lax.fori_loop(0, 8, update, 0)
            if n + 1 < STEPS:
                traces(n + 1, s)
                send_halo(n + 1, s)
            else:
                pltpu.make_async_copy(
                    F.at[s], out_hbm.at[:, pl.ds(s * PLANE, PLANE)], out_sem.at[s]
                ).start()
            parts.append(plane_sums(s))
        send_sums(n + 1, parts)

    S = wait_sums(STEPS)
    density, u, temp, heat = observables(S)
    for i, value in enumerate([density] + u + [temp] + heat):
        PR[i : i + 1] = value
    final = PR[0:8]
    for r in range(8):
        macro[:, r, :] = final[:, r * 16 : (r + 1) * 16]
    edges = weight * jnp.dot(
        S, edge[:, 256:384], preferred_element_type=F32, precision=lax.Precision.HIGHEST
    )
    incident, upward, downward = edges[4:5, 0:8], edges[3:4, 8:16], edges[4:5, 8:16]
    flux[...] = jnp.where(
        gz == 0,
        jnp.where(bottom_code == 1, SAT_DENSITY * half_flux - incident, 0.0),
        jnp.where(top_code == 2, upward - downward, 0.0),
    )

    for s in range(3):
        pltpu.make_async_copy(
            F.at[s], out_hbm.at[:, pl.ds(s * PLANE, PLANE)], out_sem.at[s]
        ).wait()
    for n in range(STEPS):
        for s in range(3):

            @pl.when(row > 0)
            def _():
                radial_copy(n, s, 0).wait_send()

            @pl.when(row < last_row)
            def _():
                radial_copy(n, s, 1).wait_send()

            axial_copy(n, s).wait_send()
    for n in range(STEPS + 1):

        def done(k, carry, n=n):
            sum_copy(n, vert, lax.rem(vert + k, vert_total), k).wait_send()
            return carry

        lax.fori_loop(1, vert_total, done, 0)


def solution(mesh):
    row_total, vert_total = mesh.shape["row"], mesh.shape["vert"]
    arrays, weight, half_flux, points = constants()

    def on_device(distribution, z_order, edge_codes):
        f = distribution.reshape(128, 3 * PLANE)
        hbm = pl.BlockSpec(memory_space=pl.ANY)
        smem = pl.BlockSpec(memory_space=pltpu.SMEM)
        vmem = pl.BlockSpec(memory_space=pltpu.VMEM)
        dma = pltpu.SemaphoreType.DMA
        new, macro, flux = pl.pallas_call(
            functools.partial(kernel, (row_total, vert_total), weight, half_flux, points),
            out_shape=(
                jax.ShapeDtypeStruct((128, 3 * PLANE), F32),
                jax.ShapeDtypeStruct((8, 8, 16), F32),
                jax.ShapeDtypeStruct((1, 8), F32),
            ),
            in_specs=[hbm, smem, smem] + [hbm] * len(arrays),
            out_specs=(hbm, vmem, vmem),
            scratch_shapes=[
                pltpu.VMEM((3, 128, PLANE), F32),
                pltpu.VMEM((3, 160, PLANE), BF16),
                pltpu.VMEM((3, 128, PLANE), BF16),
                pltpu.VMEM((3, 128, PLANE), F32),
                pltpu.VMEM((3, 256, PLANE), F32),
                pltpu.VMEM((3, 2, 256, 160), BF16),
                pltpu.VMEM((128, PLANE), F32),
                pltpu.VMEM((128, PLANE), F32),
                pltpu.VMEM((128, PLANE), F32),
                pltpu.VMEM((128, 128), F32),
                pltpu.VMEM((128, 128), F32),
            ]
            + [pltpu.VMEM(x.shape, x.dtype) for x in arrays]
            + [
                pltpu.VMEM((STEPS, 3, 2, 16, HALF), F32),
                pltpu.VMEM((STEPS, 3, 8, PLANE), F32),
                pltpu.VMEM((STEPS, 3, 2, 16, HALF), F32),
                pltpu.VMEM((STEPS, 3, 8, PLANE), F32),
                pltpu.VMEM((STEPS + 1, 16, 128), F32),
                pltpu.VMEM((STEPS + 1, vert_total, 16, 128), F32),
                dma((3,)),
                dma((len(arrays),)),
                dma((3,)),
                dma((STEPS, 3, 2)),
                dma((STEPS, 3, 2)),
                dma((STEPS, 3)),
                dma((STEPS, 3)),
                dma((STEPS + 1, vert_total)),
                dma((STEPS + 1, vert_total)),
            ],
            compiler_params=pltpu.CompilerParams(
                collective_id=0, has_side_effects=True, vmem_limit_bytes=56 * 1024 * 1024
            ),
        )(f, z_order, edge_codes, *arrays)
        return new.reshape(distribution.shape), macro, flux

    in_specs = (P("row", "gz", "vert"), P("vert"), P(None, "row"))
    out_specs = (P("row", "gz", "vert"), P(None, "row", "gz"), P("gz", "row"))
    return jax.shard_map(
        on_device, mesh=mesh, in_specs=in_specs, out_specs=out_specs, check_vma=False
    )
```

```python
import functools
import math

import jax
import jax.numpy as jnp
import ml_dtypes
import numpy as np
from jax import lax
from jax.experimental import pallas as pl
from jax.experimental.pallas import tpu as pltpu
from jax.sharding import PartitionSpec as P

NODES = 8
NVR = 48
NVT = 48
NVZ = 48
STEPS = 2

ELEMENT_WIDTH = 4.0
TIME_STEP = 0.001
KNUDSEN = 0.005
VISCOUS_RATIO = 2.0 / 3.0
SAT_DENSITY = 1.5
SPEED_LIMIT = 5.0

PLANE = NVR * NVT
HALF = PLANE // 2
GRID_STEP = 2 * SPEED_LIMIT / NVR
UNIT = GRID_STEP / 2
MESH_IDS = pl.DeviceIdType.MESH
F32 = jnp.float32
BF16 = jnp.bfloat16


def legendre_pair(position, point_count):
    previous = 1.0
    current = position
    for degree in range(2, point_count + 1):
        previous, current = (
            current,
            ((2 * degree - 1) * position * current - (degree - 1) * previous) / degree,
        )
    slope = point_count * (position * current - previous) / (position * position - 1.0)
    return (current, slope)


def dg_tables(point_count):
    point_list = []
    weight_list = []
    for number in range(point_count):
        position = math.cos(math.pi * (number + 0.75) / (point_count + 0.5))
        for sweep in range(60):
            value, slope = legendre_pair(position, point_count)
            position = position - value / slope
        value, slope = legendre_pair(position, point_count)
        point_list.append(position)
        weight_list.append(2.0 / ((1.0 - position * position) * slope * slope))
    point_list = point_list[::-1]
    weight_list = weight_list[::-1]
    products = []
    for row_number in range(point_count):
        product_value = 1.0
        for other in range(point_count):
            if other != row_number:
                product_value = product_value * (point_list[row_number] - point_list[other])
        products.append(product_value)
    derivative_rows = []
    for row_number in range(point_count):
        entries = []
        for column in range(point_count):
            if column == row_number:
                total_value = 0.0
                for other in range(point_count):
                    if other != row_number:
                        total_value = total_value + 1.0 / (
                            point_list[row_number] - point_list[other]
                        )
                entries.append(total_value)
            else:
                entries.append(
                    products[row_number]
                    / products[column]
                    / (point_list[row_number] - point_list[column])
                )
        derivative_rows.append(entries)
    right_list = []
    left_list = []
    for column in range(point_count):
        right_value = 1.0
        left_value = 1.0
        for other in range(point_count):
            if other != column:
                right_value = right_value * (1.0 - point_list[other])
                left_value = left_value * (-1.0 - point_list[other])
        right_list.append(right_value / products[column])
        left_list.append(left_value / products[column])
    points = np.array(point_list)
    quad_weights = np.array(weight_list)
    derivative = np.array(derivative_rows)
    end_right = np.array(right_list)
    end_left = np.array(left_list)
    return (
        points,
        derivative,
        end_right / quad_weights,
        end_left / quad_weights,
        end_right,
        end_left,
    )


def speed_grid(point_count):
    return -SPEED_LIMIT + (np.arange(point_count) + 0.5) * (2.0 * SPEED_LIMIT / point_count)


def split_exact(values, count):
    parts = []
    rest = np.asarray(values, np.float64)
    for _ in range(count):
        head = rest.astype(ml_dtypes.bfloat16).astype(np.float64)
        parts.append(head)
        rest = rest - head
    assert not np.any(rest)
    return parts


def constants():
    points, derivative, lift_right, lift_left, end_right, end_left = dg_tables(NODES)
    eye8, eye16 = np.eye(8), np.eye(16)
    scale = -TIME_STEP * 2.0 / ELEMENT_WIDTH
    plus = derivative + np.outer(lift_left, end_left)
    minus = derivative - np.outer(lift_right, end_right)
    radial = np.zeros((3, 128, 160))
    for k, (core, ghost) in enumerate(
        [(minus, lift_right), (derivative, 0 * lift_right), (plus, -lift_left)]
    ):
        radial[k, :, :128] = np.kron(core, eye16)
        radial[k, :, 128:144] = np.kron(ghost[:, None], eye16)
    up = np.zeros((16, 16))
    up[:8, :8] = plus
    up[8:, 8:] = plus
    up[8:, :8] = -np.outer(lift_left, end_right)
    down = np.zeros((16, 16))
    down[:8, :8] = minus
    down[8:, 8:] = minus
    down[:8, 8:] = np.outer(lift_right, end_left)
    outflow = down.copy()
    outflow[8:, 8:] = derivative
    none = np.zeros(16)
    up_ghost = np.concatenate([-lift_left, np.zeros(8)])
    down_ghost = np.concatenate([np.zeros(8), lift_right])
    axial = np.zeros((5, 128, 160))
    for k, (core, ghost) in enumerate(
        [(up, none), (up, up_ghost), (down, down_ghost), (down, none), (outflow, none)]
    ):
        axial[k, :, :128] = np.kron(eye8, core)
        axial[k, :, 144:152] = np.kron(eye8, ghost[:, None])
    low_first = np.concatenate([end_left, np.zeros(8)])
    high_last = np.concatenate([np.zeros(8), end_right])
    trace = np.zeros((2, 2, 32, 128))
    for g, across in enumerate([high_last, low_first]):
        for h, along in enumerate([end_left, end_right]):
            trace[g, h, :16] = np.kron(along[None, :], eye16)
            trace[g, h, 16:24] = np.kron(eye8, across[None, :])
    odd = 2.0 * np.arange(48) + 1 - 48
    nr, nt = np.repeat(odd, 48), np.tile(odd, 48)
    square = nr * nr + nt * nt
    columns = (
        [np.ones(PLANE), nr, nt]
        + split_exact(nr * nr, 2)
        + split_exact(nt * nt, 2)
        + split_exact(nr * nt, 2)
        + split_exact(nr * square, 3)
        + split_exact(nt * square, 3)
        + [np.zeros(PLANE)]
    )
    basis = np.stack(columns)
    grid = speed_grid(48)
    column = np.ones((1, 128))
    index = np.arange(48)
    turn = TIME_STEP * grid / (2 * GRID_STEP)
    rows = np.stack(
        [
            grid[:, None] * column,
            np.exp(-(grid**2) / 2)[:, None] * column,
            (-turn * grid)[:, None] * column,
            (turn * (index < 47))[:, None] * column,
            (turn * (index > 0))[:, None] * column,
        ]
    )
    ones8 = np.ones(8)
    edge = np.zeros((128, 384))
    edge[:, :128] = np.kron(eye8, np.outer(low_first, np.ones(16)))
    edge[:, 128:256] = np.kron(eye8, np.outer(high_last, np.ones(16)))
    edge[:, 256:264] = np.kron(eye8, low_first[:, None])
    edge[:, 264:272] = np.kron(eye8, high_last[:, None])
    wall = np.zeros((8, 128))
    wall[0] = np.kron(ones8, np.concatenate([-scale * lift_left, np.zeros(8)]))
    wall[1] = np.kron(ones8, np.concatenate([np.zeros(8), scale * lift_right]))
    wall[2] = np.kron((1.0 + np.array(points)) / 2, np.ones(16))
    weight = GRID_STEP**3 / (2 * math.pi) ** 1.5
    half_flux = (
        weight
        * np.sum(np.exp(-(grid**2) / 2)) ** 2
        * np.sum(np.maximum(grid, 0.0) * np.exp(-(grid**2) / 2))
    )
    as_bf16 = lambda x: jnp.asarray(x.astype(np.float32).astype(ml_dtypes.bfloat16))
    as_f32 = lambda x: jnp.asarray(x.astype(np.float32))
    arrays = (
        as_bf16(scale * radial.transpose(0, 2, 1)),
        as_f32(scale * axial.transpose(0, 2, 1)),
        as_bf16(trace),
        as_bf16(basis),
        as_f32(rows),
        as_f32(edge),
        as_f32(wall),
    )
    return arrays, float(weight), float(half_flux)


def kernel(
    sizes, weight, half_flux,
    f_hbm, order, codes, radial_hbm, axial_hbm, trace_hbm, basis_hbm, rows_hbm, edge_hbm, wall_hbm,
    out, macro, flux,
    RAW, F, X, LO, PART, TOUT, W, TURN, BYT, BYR, PR,
    radial, axial, trace, basis, rows, edge, wall,
    trR, trA, ghR, ghA, mine, ARB,
    load_sem, const_sem,
    rs_send, rs_recv, as_send, as_recv, ar_send, ar_recv,
):
    row_total, vert_total = sizes
    row, gz, vert = lax.axis_index("row"), lax.axis_index("gz"), lax.axis_index("vert")
    last_row = row_total - 1

    barrier = pltpu.get_barrier_semaphore()

    def hello(k, carry):
        peer = lax.rem(vert + k, vert_total)
        pl.semaphore_signal(barrier, inc=1, device_id=(row, gz, peer), device_id_type=MESH_IDS)
        return carry

    lax.fori_loop(1, vert_total, hello, 0)
    pl.semaphore_signal(barrier, inc=1, device_id=(row, 1 - gz, vert), device_id_type=MESH_IDS)

    @pl.when(row > 0)
    def _():
        pl.semaphore_signal(barrier, inc=1, device_id=(row - 1, gz, vert), device_id_type=MESH_IDS)

    @pl.when(row < last_row)
    def _():
        pl.semaphore_signal(barrier, inc=1, device_id=(row + 1, gz, vert), device_id_type=MESH_IDS)

    loads = [
        pltpu.make_async_copy(f_hbm.at[:, pl.ds(s * PLANE, PLANE)], RAW.at[s], load_sem.at[s])
        for s in range(3)
    ]
    consts = [
        pltpu.make_async_copy(src, dst, const_sem.at[k])
        for k, (src, dst) in enumerate(
            [
                (trace_hbm, trace),
                (basis_hbm, basis),
                (rows_hbm, rows),
                (radial_hbm, radial),
                (axial_hbm, axial),
                (edge_hbm, edge),
                (wall_hbm, wall),
            ]
        )
    ]
    loads[0].start()
    for copy in consts[:2]:
        copy.start()
    for copy in loads[1:]:
        copy.start()
    for copy in consts[2:]:
        copy.start()

    speeds = [(2 * order[s] - (NVZ - 1)).astype(F32) * UNIT for s in range(3)]
    bottom_code, top_code = codes[0], codes[1]
    zero16 = jnp.zeros((16, HALF), F32)

    def radial_copy(n, s, h):
        step = 1 if h else -1
        return pltpu.make_async_remote_copy(
            src_ref=trR.at[n, s, h],
            dst_ref=ghR.at[n, s, h],
            send_sem=rs_send.at[n, s, h],
            recv_sem=rs_recv.at[n, s, h],
            device_id=(row + step, gz, vert),
            device_id_type=MESH_IDS,
        )

    def axial_copy(n, s):
        return pltpu.make_async_remote_copy(
            src_ref=trA.at[n, s],
            dst_ref=ghA.at[n, s],
            send_sem=as_send.at[n, s],
            recv_sem=as_recv.at[n, s],
            device_id=(row, 1 - gz, vert),
            device_id_type=MESH_IDS,
        )

    def sum_copy(n, slot, peer, k):
        return pltpu.make_async_remote_copy(
            src_ref=mine.at[n],
            dst_ref=ARB.at[n, slot],
            send_sem=ar_send.at[n, k],
            recv_sem=ar_recv.at[n, slot],
            device_id=(row, gz, peer),
            device_id_type=MESH_IDS,
        )

    def each_peer(action):
        def body(k, carry):
            action(lax.rem(vert + k, vert_total), k)
            return carry

        lax.fori_loop(1, vert_total, body, 0)

    def send_halo(n, s):
        @pl.when(row > 0)
        def _():
            radial_copy(n, s, 0).start()

        @pl.when(row < last_row)
        def _():
            radial_copy(n, s, 1).start()

        axial_copy(n, s).start()

    over_lanes = (((1,), (1,)), ((), ()))

    def traces(n, s):
        for h in range(2):
            here = pl.ds(h * HALF, HALF)
            both = lax.dot_general(
                trace[gz, h], X[s, here, 0:128], over_lanes, preferred_element_type=F32
            )
            trR[n, s, h] = both[0:16]
            trA[n, s, :, here] = both[16:24]

    def ghost_columns(s, h, table):
        for k in range(HALF // 128):
            X[s, h * HALF + k * 128 : h * HALF + (k + 1) * 128, 128:160] = (
                table[:, k * 128 : (k + 1) * 128].T.astype(BF16)
            )

    def ghosts(n, s):
        @pl.when(row < last_row)
        def _():
            radial_copy(n, s, 0).wait_recv()

        @pl.when(row > 0)
        def _():
            radial_copy(n, s, 1).wait_recv()

        axial_copy(n, s).wait_recv()
        spare = jnp.zeros((8, HALF), F32)
        low = [ghA[n, s, :, 0:HALF], spare]
        high = [ghA[n, s, :, HALF:PLANE], spare]

        @pl.when(row < last_row)
        def _():
            ghost_columns(s, 0, jnp.concatenate([ghR[n, s, 0]] + low, axis=0))

        @pl.when(row == last_row)
        def _():
            ghost_columns(s, 0, jnp.concatenate([zero16] + low, axis=0))

        @pl.when(row > 0)
        def _():
            ghost_columns(s, 1, jnp.concatenate([ghR[n, s, 1]] + high, axis=0))

        @pl.when(row == 0)
        def _():
            own = trR[n, s, 0]
            mirror = jnp.concatenate(
                [own[:, k * NVT : (k + 1) * NVT] for k in reversed(range(NVR // 2))], axis=1
            )
            ghost_columns(s, 1, jnp.concatenate([mirror] + high, axis=0))

    def plane_sums(s):
        table = jnp.dot(basis[...], X[s, :, 0:128], preferred_element_type=F32)
        table += jnp.dot(basis[...], LO[s], preferred_element_type=F32)
        z = speeds[s]
        g = [table[i : i + 1] for i in range(15)]
        b0, br, bt = g[0], UNIT * g[1], UNIT * g[2]
        brr, btt, brt = (UNIT**2 * (g[i] + g[i + 1]) for i in (3, 5, 7))
        br3, bt3 = (UNIT**3 * (g[i] + (g[i + 1] + g[i + 2])) for i in (9, 12))
        return [
            b0,
            br,
            bt,
            jnp.maximum(z, 0.0) * b0,
            jnp.maximum(-z, 0.0) * b0,
            brr,
            btt,
            z * z * b0,
            brt,
            z * br,
            z * bt,
            br3 + z * z * br,
            bt3 + z * z * bt,
            z * (brr + btt) + (z * z * z) * b0,
        ]

    def send_sums(n, parts):
        for i in range(14):
            mine[n, i : i + 1] = parts[0][i] + (parts[1][i] + parts[2][i])
        mine[n, 14:16] = jnp.zeros((2, 128), F32)
        ARB[n, vert] = mine[n]
        each_peer(lambda peer, k: sum_copy(n, vert, peer, k).start())

    def wait_totals(n):
        each_peer(lambda peer, k: sum_copy(n, peer, peer, k).wait_recv())
        terms = [ARB[n, k] for k in range(vert_total)]
        while len(terms) > 1:
            terms = [terms[i] + terms[i + 1] for i in range(0, len(terms), 2)]
        return [terms[0][i : i + 1] for i in range(14)]

    def observables(S):
        m = S
        inv = 1.0 / m[0]
        u = [m[1] * inv, m[2] * inv, (m[3] - m[4]) * inv]
        usq = u[0] * u[0] + u[1] * u[1] + u[2] * u[2]
        tr = m[5] + m[6] + m[7]
        temp = (tr * inv - usq) / 3.0
        tensor = [[m[5], m[8], m[9]], [m[8], m[6], m[10]], [m[9], m[10], m[7]]]
        heat = []
        for i in range(3):
            mixed = tensor[i][0] * u[0] + tensor[i][1] * u[1] + tensor[i][2] * u[2]
            raw = m[11 + i] - 2.0 * mixed - u[i] * tr + (2.0 * usq * m[0]) * u[i]
            heat.append((0.5 * weight) * raw)
        return weight * m[0], u, temp, heat

    def params(S):
        density, u, temp, heat = observables(S)
        flows = jnp.concatenate([S[3], S[4], jnp.zeros((6, 128), F32)], axis=0)
        edges = jnp.dot(
            flows, edge[:, 0:256], preferred_element_type=F32, precision=lax.Precision.HIGHEST
        )
        incident = weight * edges[1:2, 0:128]
        upward = weight * edges[0:1, 128:256]
        bottom = jnp.where(bottom_code == 1, SAT_DENSITY, incident / half_flux)
        top = jnp.where(top_code == 2, 0.0, upward / half_flux)
        wall_gain = jnp.where(gz == 0, bottom * wall[0:1], top * wall[1:2])
        inv_temp = 1.0 / temp
        kappa = ((1.0 - VISCOUS_RATIO) / 5.0) * inv_temp * inv_temp / density
        rate = (TIME_STEP / KNUDSEN) * density
        peak = rate * density * inv_temp * lax.rsqrt(temp)
        PR[0:1] = 1.0 - rate
        centred = rows[0] - u[0]
        square = centred * centred
        around = [
            jnp.exp(square * (-0.5 * inv_temp)),
            centred * (kappa * heat[0]),
            square * inv_temp - 5.0,
        ]
        centred = rows[0] - u[1]
        square = centred * centred
        BYT[0] = jnp.exp(square * (-0.5 * inv_temp))
        BYT[1] = centred * (kappa * heat[1])
        BYT[2] = square * inv_temp
        for s in range(3):
            z = speeds[s]
            cz = z - u[2]
            inward = jnp.where(gz == 0, jnp.maximum(z, 0.0), jnp.minimum(z, 0.0))
            BYR[s, 0] = around[0] * (peak * jnp.exp(-0.5 * cz * cz * inv_temp))
            BYR[s, 1] = around[1] + kappa * heat[2] * cz
            BYR[s, 2] = around[2] + cz * cz * inv_temp
            BYR[s, 3] = rows[1] * (
                inward * wall_gain * jnp.exp(jnp.zeros((1, 128), F32) - 0.5 * z * z)
            )

    for n in range(STEPS):
        for s in range(3):
            F[n, s, 0:NVT] = jnp.zeros((NVT, 128), F32)
            F[n, s, NVT + PLANE :] = jnp.zeros((NVT, 128), F32)
    for copy in consts[:2]:
        copy.wait()
    parts = []
    for s in range(3):
        loads[s].wait()

        def split(r, carry, s=s):
            at = pl.ds(pl.multiple_of(r * 128, 128), 128)
            x = RAW[s, :, at].T
            F[0, s, pl.ds(pl.multiple_of(NVT + r * 128, 8), 128), :] = x
            hi = x.astype(BF16)
            X[s, at, 0:128] = hi
            LO[s, at, :] = (x - hi.astype(F32)).astype(BF16)
            return carry

        lax.fori_loop(0, PLANE // 128, split, 0, unroll=3)
        traces(0, s)
        if s == 0:
            peers = vert_total + (row > 0).astype(jnp.int32) + (row < last_row).astype(jnp.int32)
            pl.semaphore_wait(barrier, peers)

        send_halo(0, s)
        parts.append(plane_sums(s))
    send_sums(0, parts)

    for copy in consts[2:]:
        copy.wait()
    for s in range(3):
        z = speeds[s]
        up = jnp.where(gz == 0, axial[0], axial[1])
        down = jnp.where(gz == 0, axial[2], jnp.where(top_code == 2, axial[4], axial[3]))
        along = (z * jnp.where(z > 0, up, down)).astype(BF16)
        for h in range(2):
            W[s, h, :, 128:256] = along
        W[s, 0, :, 0:128] = radial[jnp.where(row == last_row, 1, 0)]
        W[s, 1, :, 0:128] = radial[2]

    inverse = 1.0 / ((row.astype(F32) + wall[2:3]) * ELEMENT_WIDTH)
    for k in range(3):
        TURN[k] = rows[2 + k] * inverse

    for n in range(STEPS):
        for s in range(3):
            ghosts(n, s)
            for h in range(2):
                here = pl.ds(h * HALF, HALF)
                TOUT[s, here, :] = jnp.dot(X[s, here, :], W[s, h], preferred_element_type=F32)

            def stream(a, carry, s=s):
                at = pl.ds(pl.multiple_of(a * NVT, 16), NVT)
                behind, here, ahead = (
                    F[n, s, pl.ds(pl.multiple_of((a + k) * NVT, 8), NVT), :] for k in range(3)
                )
                speed = (2 * a - (NVR - 1)).astype(F32) * UNIT
                around = TURN[1] * pltpu.roll(here, NVT - 1, 0) - TURN[2] * pltpu.roll(here, 1, 0)
                PART[s, at, :] = (
                    TURN[0] * (ahead - behind)
                    + speed * (around + TOUT[s, at, 0:128])
                    + TOUT[s, at, 128:256]
                )
                return carry

            lax.fori_loop(0, NVR, stream, 0, unroll=4)

        params(wait_totals(n))

        parts = []
        for s in range(3):

            def update(a, carry, s=s):
                at = pl.ds(pl.multiple_of(a * NVT, 16), NVT)
                own = pl.ds(pl.multiple_of((a + 1) * NVT, 8), NVT)
                peak, heat, excess, wall_row = (BYR[s, k, pl.ds(a, 1), :] for k in range(4))
                goal = (BYT[0] * peak) * (1.0 + (BYT[1] + heat) * (BYT[2] + excess))
                x = PR[0:1] * F[n, s, own, :] + PART[s, at, :] + wall_row * rows[1] + goal
                F[(n + 1) % 2, s, own, :] = x
                hi = x.astype(BF16)
                X[s, at, 0:128] = hi
                LO[s, at, :] = (x - hi.astype(F32)).astype(BF16)
                return carry

            lax.fori_loop(0, NVR, update, 0, unroll=4)
            if n + 1 < STEPS:
                traces(n + 1, s)
                send_halo(n + 1, s)
            parts.append(plane_sums(s))
        send_sums(n + 1, parts)

    for s in range(3):

        def back(r, carry, s=s):
            at = pl.ds(pl.multiple_of(r * 128, 128), 128)
            x = F[STEPS % 2, s, pl.ds(pl.multiple_of(NVT + r * 128, 8), 128), :]
            out[:, pl.ds(pl.multiple_of(s * PLANE + r * 128, 128), 128)] = x.T
            return carry

        lax.fori_loop(0, PLANE // 128, back, 0, unroll=3)
    S = wait_totals(STEPS)
    density, u, temp, heat = observables(S)
    for i, value in enumerate([density] + u + [temp] + heat):
        PR[i : i + 1] = value
    final = PR[0:8]
    for r in range(8):
        macro[:, r, :] = final[:, r * 16 : (r + 1) * 16]
    flows = jnp.concatenate([S[3], S[4], jnp.zeros((6, 128), F32)], axis=0)
    edges = weight * jnp.dot(
        flows, edge[:, 256:384], preferred_element_type=F32, precision=lax.Precision.HIGHEST
    )
    incident, upward, downward = edges[1:2, 0:8], edges[0:1, 8:16], edges[1:2, 8:16]
    flux[...] = jnp.where(
        gz == 0,
        jnp.where(bottom_code == 1, SAT_DENSITY * half_flux - incident, 0.0),
        jnp.where(top_code == 2, upward - downward, 0.0),
    )

    for n in range(STEPS):
        for s in range(3):

            @pl.when(row > 0)
            def _():
                radial_copy(n, s, 0).wait_send()

            @pl.when(row < last_row)
            def _():
                radial_copy(n, s, 1).wait_send()

            axial_copy(n, s).wait_send()
    for n in range(STEPS + 1):
        each_peer(lambda peer, k, n=n: sum_copy(n, vert, peer, k).wait_send())


def deliver(new, macro, flux, new_hbm, macro_hbm, flux_hbm, sems):
    copies = [
        pltpu.make_async_copy(src, dst, sems.at[k])
        for k, (src, dst) in enumerate([(new, new_hbm), (macro, macro_hbm), (flux, flux_hbm)])
    ]
    for copy in copies:
        copy.start()
    for copy in copies:
        copy.wait()


def solution(mesh):
    row_total, vert_total = mesh.shape["row"], mesh.shape["vert"]
    arrays, weight, half_flux = constants()

    def on_device(distribution, z_order, edge_codes):
        f = distribution.reshape(128, 3 * PLANE)
        outs = (
            jax.ShapeDtypeStruct((128, 3 * PLANE), F32),
            jax.ShapeDtypeStruct((8, 8, 16), F32),
            jax.ShapeDtypeStruct((1, 8), F32),
        )
        hbm = pl.BlockSpec(memory_space=pl.ANY)
        smem = pl.BlockSpec(memory_space=pltpu.SMEM)
        vmem = pl.BlockSpec(memory_space=pltpu.VMEM)
        dma = pltpu.SemaphoreType.DMA
        new, macro, flux = pl.pallas_call(
            functools.partial(kernel, (row_total, vert_total), weight, half_flux),
            out_shape=(pltpu.VMEM(outs[0].shape, F32), outs[1], outs[2]),
            in_specs=[hbm, smem, smem] + [hbm] * len(arrays),
            out_specs=(vmem, vmem, vmem),
            scratch_shapes=[
                pltpu.VMEM((3, 128, PLANE), F32),
                pltpu.VMEM((2, 3, PLANE + 2 * NVT, 128), F32),
                pltpu.VMEM((3, PLANE, 160), BF16),
                pltpu.VMEM((3, PLANE, 128), BF16),
                pltpu.VMEM((3, PLANE, 128), F32),
                pltpu.VMEM((3, PLANE, 256), F32),
                pltpu.VMEM((3, 2, 160, 256), BF16),
                pltpu.VMEM((3, NVT, 128), F32),
                pltpu.VMEM((3, NVT, 128), F32),
                pltpu.VMEM((3, 4, NVR, 128), F32),
                pltpu.VMEM((8, 128), F32),
            ]
            + [pltpu.VMEM(x.shape, x.dtype) for x in arrays]
            + [
                pltpu.VMEM((STEPS, 3, 2, 16, HALF), F32),
                pltpu.VMEM((STEPS, 3, 8, PLANE), F32),
                pltpu.VMEM((STEPS, 3, 2, 16, HALF), F32),
                pltpu.VMEM((STEPS, 3, 8, PLANE), F32),
                pltpu.VMEM((STEPS + 1, 16, 128), F32),
                pltpu.VMEM((STEPS + 1, vert_total, 16, 128), F32),
                dma((3,)),
                dma((len(arrays),)),
                dma((STEPS, 3, 2)),
                dma((STEPS, 3, 2)),
                dma((STEPS, 3)),
                dma((STEPS, 3)),
                dma((STEPS + 1, vert_total)),
                dma((STEPS + 1, vert_total)),
            ],
            compiler_params=pltpu.CompilerParams(
                collective_id=0, has_side_effects=True, vmem_limit_bytes=52 * 1024 * 1024
            ),
        )(f, z_order, edge_codes.reshape(2), *arrays)
        hold = lambda x: pltpu.with_memory_space_constraint(x, pltpu.VMEM)
        new, macro, flux = pl.pallas_call(
            deliver,
            out_shape=outs,
            in_specs=[vmem, vmem, vmem],
            out_specs=(hbm, hbm, hbm),
            scratch_shapes=[dma((3,))],
        )(hold(new), macro, flux)
        return new.reshape(distribution.shape), macro, flux

    in_specs = (P("row", "gz", "vert"), P("vert"), P(None, "row"))
    out_specs = (P("row", "gz", "vert"), P(None, "row", "gz"), P("gz", "row"))
    return jax.shard_map(
        on_device, mesh=mesh, in_specs=in_specs, out_specs=out_specs, check_vma=False
    )
```

```python
import functools
import math

import jax
import jax.numpy as jnp
import ml_dtypes
import numpy as np
from jax import lax
from jax.experimental import pallas as pl
from jax.experimental.pallas import tpu as pltpu
from jax.sharding import PartitionSpec as P

NODES = 8
NVR = 48
NVT = 48
NVZ = 48
STEPS = 2

ELEMENT_WIDTH = 4.0
TIME_STEP = 0.001
KNUDSEN = 0.005
VISCOUS_RATIO = 2.0 / 3.0
SAT_DENSITY = 1.5
SPEED_LIMIT = 5.0

PLANE = NVR * NVT
HALF = PLANE // 2
GRID_STEP = 2 * SPEED_LIMIT / NVR
UNIT = GRID_STEP / 2
MESH_IDS = pl.DeviceIdType.MESH
F32 = jnp.float32
BF16 = jnp.bfloat16


def legendre_pair(position, point_count):
    previous = 1.0
    current = position
    for degree in range(2, point_count + 1):
        previous, current = (
            current,
            ((2 * degree - 1) * position * current - (degree - 1) * previous) / degree,
        )
    slope = point_count * (position * current - previous) / (position * position - 1.0)
    return (current, slope)


def dg_tables(point_count):
    point_list = []
    weight_list = []
    for number in range(point_count):
        position = math.cos(math.pi * (number + 0.75) / (point_count + 0.5))
        for sweep in range(60):
            value, slope = legendre_pair(position, point_count)
            position = position - value / slope
        value, slope = legendre_pair(position, point_count)
        point_list.append(position)
        weight_list.append(2.0 / ((1.0 - position * position) * slope * slope))
    point_list = point_list[::-1]
    weight_list = weight_list[::-1]
    products = []
    for row_number in range(point_count):
        product_value = 1.0
        for other in range(point_count):
            if other != row_number:
                product_value = product_value * (point_list[row_number] - point_list[other])
        products.append(product_value)
    derivative_rows = []
    for row_number in range(point_count):
        entries = []
        for column in range(point_count):
            if column == row_number:
                total_value = 0.0
                for other in range(point_count):
                    if other != row_number:
                        total_value = total_value + 1.0 / (
                            point_list[row_number] - point_list[other]
                        )
                entries.append(total_value)
            else:
                entries.append(
                    products[row_number]
                    / products[column]
                    / (point_list[row_number] - point_list[column])
                )
        derivative_rows.append(entries)
    right_list = []
    left_list = []
    for column in range(point_count):
        right_value = 1.0
        left_value = 1.0
        for other in range(point_count):
            if other != column:
                right_value = right_value * (1.0 - point_list[other])
                left_value = left_value * (-1.0 - point_list[other])
        right_list.append(right_value / products[column])
        left_list.append(left_value / products[column])
    points = np.array(point_list)
    quad_weights = np.array(weight_list)
    derivative = np.array(derivative_rows)
    end_right = np.array(right_list)
    end_left = np.array(left_list)
    return (
        points,
        derivative,
        end_right / quad_weights,
        end_left / quad_weights,
        end_right,
        end_left,
    )


def speed_grid(point_count):
    return -SPEED_LIMIT + (np.arange(point_count) + 0.5) * (2.0 * SPEED_LIMIT / point_count)


def split_exact(values, count):
    parts = []
    rest = np.asarray(values, np.float64)
    for _ in range(count):
        head = rest.astype(ml_dtypes.bfloat16).astype(np.float64)
        parts.append(head)
        rest = rest - head
    assert not np.any(rest)
    return parts


def constants():
    points, derivative, lift_right, lift_left, end_right, end_left = dg_tables(NODES)
    eye8, eye16 = np.eye(8), np.eye(16)
    scale = -TIME_STEP * 2.0 / ELEMENT_WIDTH
    plus = derivative + np.outer(lift_left, end_left)
    minus = derivative - np.outer(lift_right, end_right)
    radial = np.zeros((3, 128, 256))
    for k, (core, ghost) in enumerate(
        [(minus, lift_right), (derivative, 0 * lift_right), (plus, -lift_left)]
    ):
        radial[k, :, :128] = np.kron(core, eye16)
        first = 160 if k == 2 else 128
        radial[k, :, first : first + 16] = np.kron(ghost[:, None], eye16)
    up = np.zeros((16, 16))
    up[:8, :8] = plus
    up[8:, 8:] = plus
    up[8:, :8] = -np.outer(lift_left, end_right)
    down = np.zeros((16, 16))
    down[:8, :8] = minus
    down[8:, 8:] = minus
    down[:8, 8:] = np.outer(lift_right, end_left)
    outflow = down.copy()
    outflow[8:, 8:] = derivative
    none = np.zeros(16)
    up_ghost = np.concatenate([-lift_left, np.zeros(8)])
    down_ghost = np.concatenate([np.zeros(8), lift_right])
    axial = np.zeros((5, 128, 160))
    for k, (core, ghost) in enumerate(
        [(up, none), (up, up_ghost), (down, down_ghost), (down, none), (outflow, none)]
    ):
        axial[k, :, :128] = np.kron(eye8, core)
        axial[k, :, 144:152] = np.kron(eye8, ghost[:, None])
    low_first = np.concatenate([end_left, np.zeros(8)])
    high_last = np.concatenate([np.zeros(8), end_right])
    trace = np.zeros((2, 2, 32, 128))
    for g, across in enumerate([high_last, low_first]):
        for h, along in enumerate([end_left, end_right]):
            trace[g, h, :16] = np.kron(along[None, :], eye16)
            trace[g, h, 16:24] = np.kron(eye8, across[None, :])
    odd = 2.0 * np.arange(48) + 1 - 48
    nr, nt = np.repeat(odd, 48), np.tile(odd, 48)
    square = nr * nr + nt * nt
    columns = (
        [np.ones(PLANE), nr, nt]
        + split_exact(nr * nr, 2)
        + split_exact(nt * nt, 2)
        + split_exact(nr * nt, 2)
        + split_exact(nr * square, 3)
        + split_exact(nt * square, 3)
        + [np.zeros(PLANE)]
    )
    basis = np.stack(columns)
    grid = speed_grid(48)
    column = np.ones((1, 128))
    index = np.arange(48)
    turn = TIME_STEP * grid / (2 * GRID_STEP)
    rows = np.stack(
        [
            grid[:, None] * column,
            np.exp(-(grid**2) / 2)[:, None] * column,
            (-turn * grid)[:, None] * column,
            (turn * (index < 47))[:, None] * column,
            (turn * (index > 0))[:, None] * column,
        ]
    )
    ones8 = np.ones(8)
    edge = np.zeros((128, 384))
    edge[:, :128] = np.kron(eye8, np.outer(low_first, np.ones(16)))
    edge[:, 128:256] = np.kron(eye8, np.outer(high_last, np.ones(16)))
    edge[:, 256:264] = np.kron(eye8, low_first[:, None])
    edge[:, 264:272] = np.kron(eye8, high_last[:, None])
    wall = np.zeros((8, 128))
    wall[0] = np.kron(ones8, np.concatenate([-scale * lift_left, np.zeros(8)]))
    wall[1] = np.kron(ones8, np.concatenate([np.zeros(8), scale * lift_right]))
    wall[2] = np.kron((1.0 + np.array(points)) / 2, np.ones(16))
    weight = GRID_STEP**3 / (2 * math.pi) ** 1.5
    half_flux = (
        weight
        * np.sum(np.exp(-(grid**2) / 2)) ** 2
        * np.sum(np.maximum(grid, 0.0) * np.exp(-(grid**2) / 2))
    )
    as_bf16 = lambda x: jnp.asarray(x.astype(np.float32).astype(ml_dtypes.bfloat16))
    as_f32 = lambda x: jnp.asarray(x.astype(np.float32))
    arrays = (
        as_bf16(scale * radial.transpose(0, 2, 1)),
        as_f32(scale * axial.transpose(0, 2, 1)),
        as_bf16(trace),
        as_bf16(basis),
        as_f32(rows),
        as_f32(edge),
        as_f32(wall),
    )
    return arrays, float(weight), float(half_flux)


def kernel(
    sizes, weight, half_flux,
    f_hbm, order, codes, radial_hbm, axial_hbm, trace_hbm, basis_hbm, rows_hbm, edge_hbm, wall_hbm,
    out, macro, flux,
    RAW, F, G, PART, TOUT, W, TURN, BYT, BYR, PR,
    radial, axial, trace, basis, rows, edge, wall,
    trR, trA, ghR, ghA, mine, ARB,
    load_sem, const_sem,
    rs_send, rs_recv, as_send, as_recv, ar_send, ar_recv,
):
    row_total, vert_total = sizes
    row, gz, vert = lax.axis_index("row"), lax.axis_index("gz"), lax.axis_index("vert")
    last_row = row_total - 1

    def load(s):
        lanes = pl.ds(pl.multiple_of(s * PLANE, 128), PLANE)
        return pltpu.make_async_copy(f_hbm.at[:, lanes], RAW.at[s], load_sem.at[s])

    consts = [
        pltpu.make_async_copy(src, dst, const_sem.at[k])
        for k, (src, dst) in enumerate(
            [
                (trace_hbm, trace),
                (basis_hbm, basis),
                (rows_hbm, rows),
                (radial_hbm, radial),
                (axial_hbm, axial),
                (edge_hbm, edge),
                (wall_hbm, wall),
            ]
        )
    ]
    load(0).start()
    for copy in consts[:2]:
        copy.start()
    load(1).start()
    load(2).start()
    for copy in consts[2:]:
        copy.start()

    barrier = pltpu.get_barrier_semaphore()

    def hello(k, carry):
        peer = lax.rem(vert + k, vert_total)
        pl.semaphore_signal(barrier, inc=1, device_id=(row, gz, peer), device_id_type=MESH_IDS)
        return carry

    lax.fori_loop(1, vert_total, hello, 0)
    pl.semaphore_signal(barrier, inc=1, device_id=(row, 1 - gz, vert), device_id_type=MESH_IDS)

    @pl.when(row > 0)
    def _():
        pl.semaphore_signal(barrier, inc=1, device_id=(row - 1, gz, vert), device_id_type=MESH_IDS)

    @pl.when(row < last_row)
    def _():
        pl.semaphore_signal(barrier, inc=1, device_id=(row + 1, gz, vert), device_id_type=MESH_IDS)

    speeds = [(2 * order[s] - (NVZ - 1)).astype(F32) * UNIT for s in range(3)]
    bottom_code, top_code = codes[0], codes[1]
    for n in range(STEPS):
        for s in range(3):
            F[n, s, 0:NVT] = jnp.zeros((NVT, 128), F32)
            F[n, s, NVT + PLANE :] = jnp.zeros((NVT, 128), F32)
    for s in range(3):
        G[s, :, 64:128] = jnp.zeros((HALF, 64), F32)

    @pl.when(row == last_row)
    def _():
        for n in range(STEPS):
            for s in range(3):
                ghR[n, s, 0] = jnp.zeros((16, HALF), F32)


    def radial_copy(n, s, h):
        step = 1 if h else -1
        return pltpu.make_async_remote_copy(
            src_ref=trR.at[n, s, h],
            dst_ref=ghR.at[n, s, h],
            send_sem=rs_send.at[n, s, h],
            recv_sem=rs_recv.at[n, s, h],
            device_id=(row + step, gz, vert),
            device_id_type=MESH_IDS,
        )

    def axial_copy(n, s):
        return pltpu.make_async_remote_copy(
            src_ref=trA.at[n, s],
            dst_ref=ghA.at[n, s],
            send_sem=as_send.at[n, s],
            recv_sem=as_recv.at[n, s],
            device_id=(row, 1 - gz, vert),
            device_id_type=MESH_IDS,
        )

    def sum_copy(n, slot, peer, k):
        return pltpu.make_async_remote_copy(
            src_ref=mine.at[n],
            dst_ref=ARB.at[n, slot],
            send_sem=ar_send.at[n, k],
            recv_sem=ar_recv.at[n, slot],
            device_id=(row, gz, peer),
            device_id_type=MESH_IDS,
        )

    def each_peer(action):
        def body(k, carry):
            action(lax.rem(vert + k, vert_total), k)
            return carry

        lax.fori_loop(1, vert_total, body, 0)

    def send_halo(n, s):
        @pl.when(row > 0)
        def _():
            radial_copy(n, s, 0).start()

        @pl.when(row < last_row)
        def _():
            radial_copy(n, s, 1).start()

        axial_copy(n, s).start()

    over_lanes = (((1,), (1,)), ((), ()))

    def keep_traces(n, s, h, both):
        trR[n, s, h] = both[0:16]
        trA[n, s, :, h * HALF : (h + 1) * HALF] = both[16:24]

    def traces(n, s):
        for h in range(2):
            x = F[n % 2, s, NVT + h * HALF : NVT + (h + 1) * HALF, :].astype(BF16)
            both = lax.dot_general(trace[gz, h], x, over_lanes, preferred_element_type=F32)
            keep_traces(n, s, h, both)

    def plane_sums(n, s):
        total = jnp.zeros((16, 256), F32)
        for c in range(PLANE // 256):
            x = F[n % 2, s, NVT + c * 256 : NVT + (c + 1) * 256, :]
            hi = x.astype(BF16)
            lo = (x - hi.astype(F32)).astype(BF16)
            total += jnp.dot(
                basis[:, c * 256 : (c + 1) * 256],
                jnp.concatenate([hi, lo], axis=1),
                preferred_element_type=F32,
            )
        return combine(s, total)

    def ghosts(n, s):
        @pl.when(row < last_row)
        def _():
            radial_copy(n, s, 0).wait_recv()

        @pl.when(row > 0)
        def _():
            radial_copy(n, s, 1).wait_recv()

        @pl.when(row == 0)
        def _():
            own = trR[n, s, 0]
            ghR[n, s, 1] = jnp.concatenate(
                [own[:, k * NVT : (k + 1) * NVT] for k in reversed(range(NVR // 2))], axis=1
            )

        axial_copy(n, s).wait_recv()
        spare = jnp.zeros((8, 128), F32)

        def turn(k, carry):
            low = pl.ds(pl.multiple_of(k * 128, 128), 128)
            high = pl.ds(pl.multiple_of(HALF + k * 128, 128), 128)
            table = [ghR[n, s, 0, :, low], ghA[n, s, :, low], spare]
            table += [ghR[n, s, 1, :, low], ghA[n, s, :, high], spare]
            G[s, low, 0:64] = jnp.concatenate(table, axis=0).T
            return carry

        lax.fori_loop(0, HALF // 128, turn, 0, unroll=9)

    def combine(s, total):
        table = total[:, 0:128] + total[:, 128:256]
        z = (2 * order[s] - (NVZ - 1)).astype(F32) * UNIT
        g = [table[i : i + 1] for i in range(15)]
        b0, br, bt = g[0], UNIT * g[1], UNIT * g[2]
        brr, btt, brt = (UNIT**2 * (g[i] + g[i + 1]) for i in (3, 5, 7))
        br3, bt3 = (UNIT**3 * (g[i] + (g[i + 1] + g[i + 2])) for i in (9, 12))
        return [
            b0,
            br,
            bt,
            jnp.maximum(z, 0.0) * b0,
            jnp.maximum(-z, 0.0) * b0,
            brr,
            btt,
            z * z * b0,
            brt,
            z * br,
            z * bt,
            br3 + z * z * br,
            bt3 + z * z * bt,
            z * (brr + btt) + (z * z * z) * b0,
        ]

    def send_sums(n, parts):
        for i in range(14):
            mine[n, i : i + 1] = parts[i]
        mine[n, 14:16] = jnp.zeros((2, 128), F32)
        ARB[n, vert] = mine[n]
        each_peer(lambda peer, k: sum_copy(n, vert, peer, k).start())

    def wait_totals(n):
        each_peer(lambda peer, k: sum_copy(n, peer, peer, k).wait_recv())
        terms = [ARB[n, k] for k in range(vert_total)]
        while len(terms) > 1:
            terms = [terms[i] + terms[i + 1] for i in range(0, len(terms), 2)]
        return [terms[0][i : i + 1] for i in range(14)]

    def observables(S):
        m = S
        inv = 1.0 / m[0]
        u = [m[1] * inv, m[2] * inv, (m[3] - m[4]) * inv]
        usq = u[0] * u[0] + u[1] * u[1] + u[2] * u[2]
        tr = m[5] + m[6] + m[7]
        temp = (tr * inv - usq) / 3.0
        tensor = [[m[5], m[8], m[9]], [m[8], m[6], m[10]], [m[9], m[10], m[7]]]
        heat = []
        for i in range(3):
            mixed = tensor[i][0] * u[0] + tensor[i][1] * u[1] + tensor[i][2] * u[2]
            raw = m[11 + i] - 2.0 * mixed - u[i] * tr + (2.0 * usq * m[0]) * u[i]
            heat.append((0.5 * weight) * raw)
        return weight * m[0], u, temp, heat

    def params(S):
        density, u, temp, heat = observables(S)
        flows = jnp.concatenate([S[3], S[4], jnp.zeros((6, 128), F32)], axis=0)
        edges = jnp.dot(
            flows, edge[:, 0:256], preferred_element_type=F32, precision=lax.Precision.HIGHEST
        )
        incident = weight * edges[1:2, 0:128]
        upward = weight * edges[0:1, 128:256]
        bottom = jnp.where(bottom_code == 1, SAT_DENSITY, incident / half_flux)
        top = jnp.where(top_code == 2, 0.0, upward / half_flux)
        wall_gain = jnp.where(gz == 0, bottom * wall[0:1], top * wall[1:2])
        inv_temp = 1.0 / temp
        kappa = ((1.0 - VISCOUS_RATIO) / 5.0) * inv_temp * inv_temp / density
        rate = (TIME_STEP / KNUDSEN) * density
        peak = rate * density * inv_temp * lax.rsqrt(temp)
        PR[0:1] = 1.0 - rate
        centred = rows[0] - u[0]
        square = centred * centred
        around = [
            jnp.exp(square * (-0.5 * inv_temp)),
            centred * (kappa * heat[0]),
            square * inv_temp - 5.0,
        ]
        centred = rows[0] - u[1]
        square = centred * centred
        BYT[0] = jnp.exp(square * (-0.5 * inv_temp))
        BYT[1] = centred * (kappa * heat[1])
        BYT[2] = square * inv_temp
        for s in range(3):
            z = speeds[s]
            cz = z - u[2]
            inward = jnp.where(gz == 0, jnp.maximum(z, 0.0), jnp.minimum(z, 0.0))
            BYR[s, 0] = around[0] * (peak * jnp.exp(-0.5 * cz * cz * inv_temp))
            BYR[s, 1] = around[1] + kappa * heat[2] * cz
            BYR[s, 2] = around[2] + cz * cz * inv_temp
            BYR[s, 3] = rows[1] * (
                inward * wall_gain * jnp.exp(jnp.zeros((1, 128), F32) - 0.5 * z * z)
            )

    for copy in consts[:2]:
        copy.wait()
    nothing = tuple(jnp.zeros((1, 128), F32) for _ in range(14))

    def add(parts, more):
        return tuple(a + b for a, b in zip(parts, more))

    def begin(s, parts):
        load(s).wait()
        for h in range(2):
            lanes = slice(h * HALF, (h + 1) * HALF)
            keep_traces(0, s, h, jnp.dot(
                trace[gz, h], RAW[s, :, lanes].astype(BF16), preferred_element_type=F32
            ))

        @pl.when(s == 0)
        def _():
            peers = vert_total + (row > 0).astype(jnp.int32) + (row < last_row).astype(jnp.int32)
            pl.semaphore_wait(barrier, peers)

        @pl.when(s < 2)
        def _():
            send_halo(0, s)

        def split(r, carry):
            at = pl.ds(pl.multiple_of(r * 128, 128), 128)
            F[0, s, pl.ds(pl.multiple_of(NVT + r * 128, 8), 128), :] = RAW[s, :, at].T
            return carry

        lax.fori_loop(0, PLANE // 128, split, 0, unroll=9)
        return add(parts, plane_sums(0, s))

    send_sums(0, lax.fori_loop(0, 3, begin, nothing))
    send_halo(0, 2)

    for copy in consts[2:]:
        copy.wait()
    for s in range(3):
        z = speeds[s]
        up = jnp.where(gz == 0, axial[0], axial[1])
        down = jnp.where(gz == 0, axial[2], jnp.where(top_code == 2, axial[4], axial[3]))
        along = (z * jnp.where(z > 0, up, down)).astype(BF16)
        for h in range(2):
            W[s, h, 0:128, 128:256] = along[0:128]
            W[s, h, 128:256, 128:256] = jnp.zeros((128, 128), BF16)
            W[s, h, 128 + 32 * h : 160 + 32 * h, 128:256] = along[128:160]
        W[s, 0, :, 0:128] = radial[jnp.where(row == last_row, 1, 0)]
        W[s, 1, :, 0:128] = radial[2]

    inverse = 1.0 / ((row.astype(F32) + wall[2:3]) * ELEMENT_WIDTH)
    for k in range(3):
        TURN[k] = rows[2 + k] * inverse

    for n in range(STEPS):
        def move(s, none, n=n):
            ghosts(n, s)

            for h in range(2):
                x = F[n, s, NVT + h * HALF : NVT + (h + 1) * HALF, :].astype(BF16)
                operand = jnp.concatenate([x, G[s].astype(BF16)], axis=1)
                TOUT[s, pl.ds(h * HALF, HALF), :] = jnp.dot(
                    operand, W[s, h], preferred_element_type=F32
                )

            def stream(a, carry):
                at = pl.ds(pl.multiple_of(a * NVT, 16), NVT)
                behind, ahead = (
                    F[n, s, pl.ds(pl.multiple_of((a + k) * NVT, 8), NVT), :] for k in (0, 2)
                )
                speed = (2 * a - (NVR - 1)).astype(F32) * UNIT
                base = (a + 1) * NVT
                around = (
                    TURN[1] * F[n, s, pl.ds(base + 1, NVT), :]
                    - TURN[2] * F[n, s, pl.ds(base - 1, NVT), :]
                )
                PART[s, at, :] = (
                    TURN[0] * (ahead - behind)
                    + speed * (around + TOUT[s, at, 0:128])
                    + TOUT[s, at, 128:256]
                )
                return carry

            lax.fori_loop(0, NVR, stream, 0, unroll=4)
            return none

        lax.fori_loop(0, 3, move, 0)
        params(wait_totals(n))

        def renew(s, parts, n=n):
            def update(a, carry):
                at = pl.ds(pl.multiple_of(a * NVT, 16), NVT)
                own = pl.ds(pl.multiple_of((a + 1) * NVT, 8), NVT)
                peak, heat, excess, wall_row = (BYR[s, k, pl.ds(a, 1), :] for k in range(4))
                goal = (BYT[0] * peak) * (1.0 + (BYT[1] + heat) * (BYT[2] + excess))
                F[(n + 1) % 2, s, own, :] = (
                    PR[0:1] * F[n, s, own, :] + PART[s, at, :] + wall_row * rows[1] + goal
                )
                return carry

            lax.fori_loop(0, NVR, update, 0, unroll=4)
            if n + 1 < STEPS:
                traces(n + 1, s)

                @pl.when(s < 2)
                def _():
                    send_halo(n + 1, s)

            return add(parts, plane_sums(n + 1, s))

        send_sums(n + 1, lax.fori_loop(0, 3, renew, nothing))
        if n + 1 < STEPS:
            send_halo(n + 1, 2)

    def back(r, carry):
        for s in range(3):
            x = F[STEPS % 2, s, pl.ds(pl.multiple_of(NVT + r * 128, 8), 128), :]
            out[:, pl.ds(pl.multiple_of(s * PLANE + r * 128, 128), 128)] = x.T
        return carry

    lax.fori_loop(0, PLANE // 128, back, 0, unroll=3)
    S = wait_totals(STEPS)
    density, u, temp, heat = observables(S)
    for i, value in enumerate([density] + u + [temp] + heat):
        PR[i : i + 1] = value
    final = PR[0:8]
    for r in range(8):
        macro[:, r, :] = final[:, r * 16 : (r + 1) * 16]
    flows = jnp.concatenate([S[3], S[4], jnp.zeros((6, 128), F32)], axis=0)
    edges = weight * jnp.dot(
        flows, edge[:, 256:384], preferred_element_type=F32, precision=lax.Precision.HIGHEST
    )
    incident, upward, downward = edges[1:2, 0:8], edges[0:1, 8:16], edges[1:2, 8:16]
    flux[...] = jnp.where(
        gz == 0,
        jnp.where(bottom_code == 1, SAT_DENSITY * half_flux - incident, 0.0),
        jnp.where(top_code == 2, upward - downward, 0.0),
    )

    for n in range(STEPS):
        for s in range(3):

            @pl.when(row > 0)
            def _():
                radial_copy(n, s, 0).wait_send()

            @pl.when(row < last_row)
            def _():
                radial_copy(n, s, 1).wait_send()

            axial_copy(n, s).wait_send()
    for n in range(STEPS + 1):
        each_peer(lambda peer, k, n=n: sum_copy(n, vert, peer, k).wait_send())


def deliver(new, macro, flux, new_hbm, macro_hbm, flux_hbm, sems):
    copies = [
        pltpu.make_async_copy(src, dst, sems.at[k])
        for k, (src, dst) in enumerate([(new, new_hbm), (macro, macro_hbm), (flux, flux_hbm)])
    ]
    for copy in copies:
        copy.start()
    for copy in copies:
        copy.wait()


def solution(mesh):
    row_total, vert_total = mesh.shape["row"], mesh.shape["vert"]
    arrays, weight, half_flux = constants()

    def on_device(distribution, z_order, edge_codes):
        f = distribution.reshape(128, 3 * PLANE)
        outs = (
            jax.ShapeDtypeStruct((128, 3 * PLANE), F32),
            jax.ShapeDtypeStruct((8, 8, 16), F32),
            jax.ShapeDtypeStruct((1, 8), F32),
        )
        hbm = pl.BlockSpec(memory_space=pl.ANY)
        smem = pl.BlockSpec(memory_space=pltpu.SMEM)
        vmem = pl.BlockSpec(memory_space=pltpu.VMEM)
        dma = pltpu.SemaphoreType.DMA
        new, macro, flux = pl.pallas_call(
            functools.partial(kernel, (row_total, vert_total), weight, half_flux),
            out_shape=(pltpu.VMEM(outs[0].shape, F32), outs[1], outs[2]),
            in_specs=[hbm, smem, smem] + [hbm] * len(arrays),
            out_specs=(vmem, vmem, vmem),
            scratch_shapes=[
                pltpu.VMEM((3, 128, PLANE), F32),
                pltpu.VMEM((2, 3, PLANE + 2 * NVT, 128), F32),
                pltpu.VMEM((3, HALF, 128), F32),
                pltpu.VMEM((3, PLANE, 128), F32),
                pltpu.VMEM((3, PLANE, 256), F32),
                pltpu.VMEM((3, 2, 256, 256), BF16),
                pltpu.VMEM((3, NVT, 128), F32),
                pltpu.VMEM((3, NVT, 128), F32),
                pltpu.VMEM((3, 4, NVR, 128), F32),
                pltpu.VMEM((8, 128), F32),
            ]
            + [pltpu.VMEM(x.shape, x.dtype) for x in arrays]
            + [
                pltpu.VMEM((STEPS, 3, 2, 16, HALF), F32),
                pltpu.VMEM((STEPS, 3, 8, PLANE), F32),
                pltpu.VMEM((STEPS, 3, 2, 16, HALF), F32),
                pltpu.VMEM((STEPS, 3, 8, PLANE), F32),
                pltpu.VMEM((STEPS + 1, 16, 128), F32),
                pltpu.VMEM((STEPS + 1, vert_total, 16, 128), F32),
                dma((3,)),
                dma((len(arrays),)),
                dma((STEPS, 3, 2)),
                dma((STEPS, 3, 2)),
                dma((STEPS, 3)),
                dma((STEPS, 3)),
                dma((STEPS + 1, vert_total)),
                dma((STEPS + 1, vert_total)),
            ],
            compiler_params=pltpu.CompilerParams(
                collective_id=0, has_side_effects=True, vmem_limit_bytes=52 * 1024 * 1024
            ),
        )(f, z_order, edge_codes.reshape(2), *arrays)
        hold = lambda x: pltpu.with_memory_space_constraint(x, pltpu.VMEM)
        new, macro, flux = pl.pallas_call(
            deliver,
            out_shape=outs,
            in_specs=[vmem, vmem, vmem],
            out_specs=(hbm, hbm, hbm),
            scratch_shapes=[dma((3,))],
        )(hold(new), macro, flux)
        return new.reshape(distribution.shape), macro, flux

    in_specs = (P("row", "gz", "vert"), P("vert"), P(None, "row"))
    out_specs = (P("row", "gz", "vert"), P(None, "row", "gz"), P("gz", "row"))
    return jax.shard_map(
        on_device, mesh=mesh, in_specs=in_specs, out_specs=out_specs, check_vma=False
    )
```

```python
import functools
import math

import jax
import jax.numpy as jnp
import ml_dtypes
import numpy as np
from jax import lax
from jax.experimental import pallas as pl
from jax.experimental.pallas import tpu as pltpu
from jax.sharding import PartitionSpec as P

NODES = 8
NVR = 48
NVT = 48
NVZ = 48
STEPS = 2

ELEMENT_WIDTH = 4.0
TIME_STEP = 0.001
KNUDSEN = 0.005
VISCOUS_RATIO = 2.0 / 3.0
SAT_DENSITY = 1.5
SPEED_LIMIT = 5.0

PLANE = NVR * NVT
HALF = PLANE // 2
GRID_STEP = 2 * SPEED_LIMIT / NVR
UNIT = GRID_STEP / 2
MESH_IDS = pl.DeviceIdType.MESH
F32 = jnp.float32
BF16 = jnp.bfloat16


def legendre_pair(position, point_count):
    previous = 1.0
    current = position
    for degree in range(2, point_count + 1):
        previous, current = (
            current,
            ((2 * degree - 1) * position * current - (degree - 1) * previous) / degree,
        )
    slope = point_count * (position * current - previous) / (position * position - 1.0)
    return (current, slope)


def dg_tables(point_count):
    point_list = []
    weight_list = []
    for number in range(point_count):
        position = math.cos(math.pi * (number + 0.75) / (point_count + 0.5))
        for sweep in range(60):
            value, slope = legendre_pair(position, point_count)
            position = position - value / slope
        value, slope = legendre_pair(position, point_count)
        point_list.append(position)
        weight_list.append(2.0 / ((1.0 - position * position) * slope * slope))
    point_list = point_list[::-1]
    weight_list = weight_list[::-1]
    products = []
    for row_number in range(point_count):
        product_value = 1.0
        for other in range(point_count):
            if other != row_number:
                product_value = product_value * (point_list[row_number] - point_list[other])
        products.append(product_value)
    derivative_rows = []
    for row_number in range(point_count):
        entries = []
        for column in range(point_count):
            if column == row_number:
                total_value = 0.0
                for other in range(point_count):
                    if other != row_number:
                        total_value = total_value + 1.0 / (
                            point_list[row_number] - point_list[other]
                        )
                entries.append(total_value)
            else:
                entries.append(
                    products[row_number]
                    / products[column]
                    / (point_list[row_number] - point_list[column])
                )
        derivative_rows.append(entries)
    right_list = []
    left_list = []
    for column in range(point_count):
        right_value = 1.0
        left_value = 1.0
        for other in range(point_count):
            if other != column:
                right_value = right_value * (1.0 - point_list[other])
                left_value = left_value * (-1.0 - point_list[other])
        right_list.append(right_value / products[column])
        left_list.append(left_value / products[column])
    points = np.array(point_list)
    quad_weights = np.array(weight_list)
    derivative = np.array(derivative_rows)
    end_right = np.array(right_list)
    end_left = np.array(left_list)
    return (
        points,
        derivative,
        end_right / quad_weights,
        end_left / quad_weights,
        end_right,
        end_left,
    )


def speed_grid(point_count):
    return -SPEED_LIMIT + (np.arange(point_count) + 0.5) * (2.0 * SPEED_LIMIT / point_count)


def split_exact(values, count):
    parts = []
    rest = np.asarray(values, np.float64)
    for _ in range(count):
        head = rest.astype(ml_dtypes.bfloat16).astype(np.float64)
        parts.append(head)
        rest = rest - head
    assert not np.any(rest)
    return parts


def constants():
    points, derivative, lift_right, lift_left, end_right, end_left = dg_tables(NODES)
    eye8, eye16 = np.eye(8), np.eye(16)
    scale = -TIME_STEP * 2.0 / ELEMENT_WIDTH
    plus = derivative + np.outer(lift_left, end_left)
    minus = derivative - np.outer(lift_right, end_right)
    radial = np.zeros((3, 128, 256))
    for k, (core, ghost) in enumerate(
        [(minus, lift_right), (derivative, 0 * lift_right), (plus, -lift_left)]
    ):
        radial[k, :, :128] = np.kron(core, eye16)
        first = 160 if k == 2 else 128
        radial[k, :, first : first + 16] = np.kron(ghost[:, None], eye16)
    up = np.zeros((16, 16))
    up[:8, :8] = plus
    up[8:, 8:] = plus
    up[8:, :8] = -np.outer(lift_left, end_right)
    down = np.zeros((16, 16))
    down[:8, :8] = minus
    down[8:, 8:] = minus
    down[:8, 8:] = np.outer(lift_right, end_left)
    outflow = down.copy()
    outflow[8:, 8:] = derivative
    none = np.zeros(16)
    up_ghost = np.concatenate([-lift_left, np.zeros(8)])
    down_ghost = np.concatenate([np.zeros(8), lift_right])
    axial = np.zeros((5, 128, 160))
    for k, (core, ghost) in enumerate(
        [(up, none), (up, up_ghost), (down, down_ghost), (down, none), (outflow, none)]
    ):
        axial[k, :, :128] = np.kron(eye8, core)
        axial[k, :, 144:152] = np.kron(eye8, ghost[:, None])
    low_first = np.concatenate([end_left, np.zeros(8)])
    high_last = np.concatenate([np.zeros(8), end_right])
    trace = np.zeros((2, 2, 32, 128))
    for g, across in enumerate([high_last, low_first]):
        for h, along in enumerate([end_left, end_right]):
            trace[g, h, :16] = np.kron(along[None, :], eye16)
            trace[g, h, 16:24] = np.kron(eye8, across[None, :])
    odd = 2.0 * np.arange(48) + 1 - 48
    nr, nt = np.repeat(odd, 48), np.tile(odd, 48)
    square = nr * nr + nt * nt
    columns = (
        [np.ones(PLANE), nr, nt]
        + split_exact(nr * nr, 2)
        + split_exact(nt * nt, 2)
        + split_exact(nr * nt, 2)
        + split_exact(nr * square, 3)
        + split_exact(nt * square, 3)
        + [np.zeros(PLANE)]
    )
    basis = np.stack(columns)
    grid = speed_grid(48)
    column = np.ones((1, 128))
    index = np.arange(48)
    turn = TIME_STEP * grid / (2 * GRID_STEP)
    rows = np.stack(
        [
            grid[:, None] * column,
            np.exp(-(grid**2) / 2)[:, None] * column,
            (-turn * grid)[:, None] * column,
            (turn * (index < 47))[:, None] * column,
            (turn * (index > 0))[:, None] * column,
        ]
    )
    ones8 = np.ones(8)
    edge = np.zeros((128, 384))
    edge[:, :128] = np.kron(eye8, np.outer(low_first, np.ones(16)))
    edge[:, 128:256] = np.kron(eye8, np.outer(high_last, np.ones(16)))
    edge[:, 256:264] = np.kron(eye8, low_first[:, None])
    edge[:, 264:272] = np.kron(eye8, high_last[:, None])
    wall = np.zeros((8, 128))
    wall[0] = np.kron(ones8, np.concatenate([-scale * lift_left, np.zeros(8)]))
    wall[1] = np.kron(ones8, np.concatenate([np.zeros(8), scale * lift_right]))
    wall[2] = np.kron((1.0 + np.array(points)) / 2, np.ones(16))
    weight = GRID_STEP**3 / (2 * math.pi) ** 1.5
    half_flux = (
        weight
        * np.sum(np.exp(-(grid**2) / 2)) ** 2
        * np.sum(np.maximum(grid, 0.0) * np.exp(-(grid**2) / 2))
    )
    as_bf16 = lambda x: jnp.asarray(x.astype(np.float32).astype(ml_dtypes.bfloat16))
    as_f32 = lambda x: jnp.asarray(x.astype(np.float32))
    arrays = (
        as_bf16(scale * radial.transpose(0, 2, 1)),
        as_f32(scale * axial.transpose(0, 2, 1)),
        as_bf16(trace),
        as_bf16(basis),
        as_f32(rows),
        as_f32(edge),
        as_f32(wall),
    )
    return arrays, float(weight), float(half_flux)


def kernel(
    sizes, weight, half_flux,
    f_hbm, order, codes, radial_hbm, axial_hbm, trace_hbm, basis_hbm, rows_hbm, edge_hbm, wall_hbm,
    out, macro, flux,
    RAW, F, G, PART, TOUT, W, TURN, BYT, BYR, PR,
    radial, axial, trace, basis, rows, edge, wall,
    trR, trA, ghR, ghA, mine, ARB,
    load_sem, const_sem,
    rs_send, rs_recv, as_send, as_recv, ar_send, ar_recv,
):
    row_total, vert_total = sizes
    row, gz, vert = lax.axis_index("row"), lax.axis_index("gz"), lax.axis_index("vert")
    last_row = row_total - 1

    def load(s):
        lanes = pl.ds(pl.multiple_of(s * PLANE, 128), PLANE)
        return pltpu.make_async_copy(f_hbm.at[:, lanes], RAW.at[s], load_sem.at[s])

    consts = [
        pltpu.make_async_copy(src, dst, const_sem.at[k])
        for k, (src, dst) in enumerate(
            [
                (trace_hbm, trace),
                (basis_hbm, basis),
                (rows_hbm, rows),
                (radial_hbm, radial),
                (axial_hbm, axial),
                (edge_hbm, edge),
                (wall_hbm, wall),
            ]
        )
    ]
    load(0).start()
    for copy in consts[:2]:
        copy.start()
    load(1).start()
    load(2).start()
    for copy in consts[2:]:
        copy.start()

    barrier = pltpu.get_barrier_semaphore()

    def hello(k, carry):
        peer = lax.rem(vert + k, vert_total)
        pl.semaphore_signal(barrier, inc=1, device_id=(row, gz, peer), device_id_type=MESH_IDS)
        return carry

    lax.fori_loop(1, vert_total, hello, 0)
    pl.semaphore_signal(barrier, inc=1, device_id=(row, 1 - gz, vert), device_id_type=MESH_IDS)

    @pl.when(row > 0)
    def _():
        pl.semaphore_signal(barrier, inc=1, device_id=(row - 1, gz, vert), device_id_type=MESH_IDS)

    @pl.when(row < last_row)
    def _():
        pl.semaphore_signal(barrier, inc=1, device_id=(row + 1, gz, vert), device_id_type=MESH_IDS)

    speeds = [(2 * order[s] - (NVZ - 1)).astype(F32) * UNIT for s in range(3)]
    bottom_code, top_code = codes[0], codes[1]
    for n in range(STEPS):
        for s in range(3):
            F[n, s, 0:NVT] = jnp.zeros((NVT, 128), F32)
            F[n, s, NVT + PLANE :] = jnp.zeros((NVT, 128), F32)
    for s in range(3):
        G[s, :, 64:128] = jnp.zeros((HALF, 64), F32)

    @pl.when(row == last_row)
    def _():
        for n in range(STEPS):
            for s in range(3):
                ghR[n, s, 0] = jnp.zeros((16, HALF), F32)


    def radial_copy(n, s, h):
        step = 1 if h else -1
        return pltpu.make_async_remote_copy(
            src_ref=trR.at[n, s, h],
            dst_ref=ghR.at[n, s, h],
            send_sem=rs_send.at[n, s, h],
            recv_sem=rs_recv.at[n, s, h],
            device_id=(row + step, gz, vert),
            device_id_type=MESH_IDS,
        )

    def axial_copy(n, s):
        return pltpu.make_async_remote_copy(
            src_ref=trA.at[n, s],
            dst_ref=ghA.at[n, s],
            send_sem=as_send.at[n, s],
            recv_sem=as_recv.at[n, s],
            device_id=(row, 1 - gz, vert),
            device_id_type=MESH_IDS,
        )

    def sum_copy(n, slot, peer, k):
        return pltpu.make_async_remote_copy(
            src_ref=mine.at[n],
            dst_ref=ARB.at[n, slot],
            send_sem=ar_send.at[n, k],
            recv_sem=ar_recv.at[n, slot],
            device_id=(row, gz, peer),
            device_id_type=MESH_IDS,
        )

    def each_peer(action):
        def body(k, carry):
            action(lax.rem(vert + k, vert_total), k)
            return carry

        lax.fori_loop(1, vert_total, body, 0, unroll=5)

    def send_halo(n, s):
        @pl.when(row > 0)
        def _():
            radial_copy(n, s, 0).start()

        @pl.when(row < last_row)
        def _():
            radial_copy(n, s, 1).start()

        axial_copy(n, s).start()

    over_lanes = (((1,), (1,)), ((), ()))

    def keep_traces(n, s, h, both):
        trR[n, s, h] = both[0:16]
        trA[n, s, :, h * HALF : (h + 1) * HALF] = both[16:24]

    def traces(n, s):
        for h in range(2):
            x = F[n % 2, s, NVT + h * HALF : NVT + (h + 1) * HALF, :].astype(BF16)
            both = lax.dot_general(trace[gz, h], x, over_lanes, preferred_element_type=F32)
            keep_traces(n, s, h, both)

    def plane_sums(n, s):
        total = jnp.zeros((16, 256), F32)
        for c in range(PLANE // 256):
            x = F[n % 2, s, NVT + c * 256 : NVT + (c + 1) * 256, :]
            hi = x.astype(BF16)
            lo = (x - hi.astype(F32)).astype(BF16)
            total += jnp.dot(
                basis[:, c * 256 : (c + 1) * 256],
                jnp.concatenate([hi, lo], axis=1),
                preferred_element_type=F32,
            )
        return combine(s, total)

    def ghosts(n, s):
        @pl.when(row < last_row)
        def _():
            radial_copy(n, s, 0).wait_recv()

        @pl.when(row > 0)
        def _():
            radial_copy(n, s, 1).wait_recv()

        @pl.when(row == 0)
        def _():
            own = trR[n, s, 0]
            ghR[n, s, 1] = jnp.concatenate(
                [own[:, k * NVT : (k + 1) * NVT] for k in reversed(range(NVR // 2))], axis=1
            )

        axial_copy(n, s).wait_recv()
        spare = jnp.zeros((8, 128), F32)

        def turn(k, carry):
            low = pl.ds(pl.multiple_of(k * 128, 128), 128)
            high = pl.ds(pl.multiple_of(HALF + k * 128, 128), 128)
            table = [ghR[n, s, 0, :, low], ghA[n, s, :, low], spare]
            table += [ghR[n, s, 1, :, low], ghA[n, s, :, high], spare]
            G[s, low, 0:64] = jnp.concatenate(table, axis=0).T
            return carry

        lax.fori_loop(0, HALF // 128, turn, 0, unroll=9)

    def combine(s, total):
        table = total[:, 0:128] + total[:, 128:256]
        z = (2 * order[s] - (NVZ - 1)).astype(F32) * UNIT
        g = [table[i : i + 1] for i in range(15)]
        b0, br, bt = g[0], UNIT * g[1], UNIT * g[2]
        brr, btt, brt = (UNIT**2 * (g[i] + g[i + 1]) for i in (3, 5, 7))
        br3, bt3 = (UNIT**3 * (g[i] + (g[i + 1] + g[i + 2])) for i in (9, 12))
        return [
            b0,
            br,
            bt,
            jnp.maximum(z, 0.0) * b0,
            jnp.maximum(-z, 0.0) * b0,
            brr,
            btt,
            z * z * b0,
            brt,
            z * br,
            z * bt,
            br3 + z * z * br,
            bt3 + z * z * bt,
            z * (brr + btt) + (z * z * z) * b0,
        ]

    def send_sums(n, parts):
        for i in range(14):
            mine[n, i : i + 1] = parts[i]
        mine[n, 14:16] = jnp.zeros((2, 128), F32)
        ARB[n, vert] = mine[n]
        each_peer(lambda peer, k: sum_copy(n, vert, peer, k).start())

    def wait_totals(n):
        each_peer(lambda peer, k: sum_copy(n, peer, peer, k).wait_recv())
        terms = [ARB[n, k] for k in range(vert_total)]
        while len(terms) > 1:
            terms = [terms[i] + terms[i + 1] for i in range(0, len(terms), 2)]
        return [terms[0][i : i + 1] for i in range(14)]

    def observables(S):
        m = S
        inv = 1.0 / m[0]
        u = [m[1] * inv, m[2] * inv, (m[3] - m[4]) * inv]
        usq = u[0] * u[0] + u[1] * u[1] + u[2] * u[2]
        tr = m[5] + m[6] + m[7]
        temp = (tr * inv - usq) / 3.0
        tensor = [[m[5], m[8], m[9]], [m[8], m[6], m[10]], [m[9], m[10], m[7]]]
        heat = []
        for i in range(3):
            mixed = tensor[i][0] * u[0] + tensor[i][1] * u[1] + tensor[i][2] * u[2]
            raw = m[11 + i] - 2.0 * mixed - u[i] * tr + (2.0 * usq * m[0]) * u[i]
            heat.append((0.5 * weight) * raw)
        return weight * m[0], u, temp, heat

    def params(S):
        density, u, temp, heat = observables(S)
        flows = jnp.concatenate([S[3], S[4], jnp.zeros((6, 128), F32)], axis=0)
        edges = jnp.dot(
            flows, edge[:, 0:256], preferred_element_type=F32, precision=lax.Precision.HIGHEST
        )
        incident = weight * edges[1:2, 0:128]
        upward = weight * edges[0:1, 128:256]
        bottom = jnp.where(bottom_code == 1, SAT_DENSITY, incident / half_flux)
        top = jnp.where(top_code == 2, 0.0, upward / half_flux)
        wall_gain = jnp.where(gz == 0, bottom * wall[0:1], top * wall[1:2])
        inv_temp = 1.0 / temp
        kappa = ((1.0 - VISCOUS_RATIO) / 5.0) * inv_temp * inv_temp / density
        rate = (TIME_STEP / KNUDSEN) * density
        peak = rate * density * inv_temp * lax.rsqrt(temp)
        PR[0:1] = 1.0 - rate
        centred = rows[0] - u[0]
        square = centred * centred
        around = [
            jnp.exp(square * (-0.5 * inv_temp)),
            centred * (kappa * heat[0]),
            square * inv_temp - 5.0,
        ]
        centred = rows[0] - u[1]
        square = centred * centred
        BYT[0] = jnp.exp(square * (-0.5 * inv_temp))
        BYT[1] = centred * (kappa * heat[1])
        BYT[2] = square * inv_temp
        for s in range(3):
            z = speeds[s]
            cz = z - u[2]
            inward = jnp.where(gz == 0, jnp.maximum(z, 0.0), jnp.minimum(z, 0.0))
            BYR[s, 0] = around[0] * (peak * jnp.exp(-0.5 * cz * cz * inv_temp))
            BYR[s, 1] = around[1] + kappa * heat[2] * cz
            BYR[s, 2] = around[2] + cz * cz * inv_temp
            BYR[s, 3] = rows[1] * (
                inward * wall_gain * jnp.exp(jnp.zeros((1, 128), F32) - 0.5 * z * z)
            )

    for copy in consts[:2]:
        copy.wait()
    nothing = tuple(jnp.zeros((1, 128), F32) for _ in range(14))

    def add(parts, more):
        return tuple(a + b for a, b in zip(parts, more))

    def begin(s, parts):
        load(s).wait()
        for h in range(2):
            lanes = slice(h * HALF, (h + 1) * HALF)
            keep_traces(0, s, h, jnp.dot(
                trace[gz, h], RAW[s, :, lanes].astype(BF16), preferred_element_type=F32
            ))

        @pl.when(s == 0)
        def _():
            peers = vert_total + (row > 0).astype(jnp.int32) + (row < last_row).astype(jnp.int32)
            pl.semaphore_wait(barrier, peers)

        @pl.when(s < 2)
        def _():
            send_halo(0, s)

        def split(r, carry):
            at = pl.ds(pl.multiple_of(r * 128, 128), 128)
            F[0, s, pl.ds(pl.multiple_of(NVT + r * 128, 8), 128), :] = RAW[s, :, at].T
            return carry

        lax.fori_loop(0, PLANE // 128, split, 0, unroll=9)
        return add(parts, plane_sums(0, s))

    send_sums(0, lax.fori_loop(0, 3, begin, nothing))
    send_halo(0, 2)

    for copy in consts[2:]:
        copy.wait()
    for s in range(3):
        z = speeds[s]
        up = jnp.where(gz == 0, axial[0], axial[1])
        down = jnp.where(gz == 0, axial[2], jnp.where(top_code == 2, axial[4], axial[3]))
        along = (z * jnp.where(z > 0, up, down)).astype(BF16)
        for h in range(2):
            W[s, h, 0:128, 128:256] = along[0:128]
            W[s, h, 128:256, 128:256] = jnp.zeros((128, 128), BF16)
            W[s, h, 128 + 32 * h : 160 + 32 * h, 128:256] = along[128:160]
        W[s, 0, :, 0:128] = radial[jnp.where(row == last_row, 1, 0)]
        W[s, 1, :, 0:128] = radial[2]

    inverse = 1.0 / ((row.astype(F32) + wall[2:3]) * ELEMENT_WIDTH)
    for k in range(3):
        TURN[k] = rows[2 + k] * inverse

    for n in range(STEPS):
        def move(s, none, n=n):
            ghosts(n, s)

            for h in range(2):
                x = F[n, s, NVT + h * HALF : NVT + (h + 1) * HALF, :].astype(BF16)
                operand = jnp.concatenate([x, G[s].astype(BF16)], axis=1)
                TOUT[s, pl.ds(h * HALF, HALF), :] = jnp.dot(
                    operand, W[s, h], preferred_element_type=F32
                )

            def stream(a, carry):
                at = pl.ds(pl.multiple_of(a * NVT, 16), NVT)
                behind, ahead = (
                    F[n, s, pl.ds(pl.multiple_of((a + k) * NVT, 8), NVT), :] for k in (0, 2)
                )
                speed = (2 * a - (NVR - 1)).astype(F32) * UNIT
                base = (a + 1) * NVT
                around = (
                    TURN[1] * F[n, s, pl.ds(base + 1, NVT), :]
                    - TURN[2] * F[n, s, pl.ds(base - 1, NVT), :]
                )
                PART[s, at, :] = (
                    TURN[0] * (ahead - behind)
                    + speed * (around + TOUT[s, at, 0:128])
                    + TOUT[s, at, 128:256]
                )
                return carry

            lax.fori_loop(0, NVR, stream, 0, unroll=8)
            return none

        lax.fori_loop(0, 3, move, 0)
        params(wait_totals(n))

        def renew(s, parts, n=n):
            def update(a, carry):
                at = pl.ds(pl.multiple_of(a * NVT, 16), NVT)
                own = pl.ds(pl.multiple_of((a + 1) * NVT, 8), NVT)
                peak, heat, excess, wall_row = (BYR[s, k, pl.ds(a, 1), :] for k in range(4))
                goal = (BYT[0] * peak) * (1.0 + (BYT[1] + heat) * (BYT[2] + excess))
                F[(n + 1) % 2, s, own, :] = (
                    PR[0:1] * F[n, s, own, :] + PART[s, at, :] + wall_row * rows[1] + goal
                )
                return carry

            lax.fori_loop(0, NVR, update, 0, unroll=8)
            if n + 1 < STEPS:
                traces(n + 1, s)

                @pl.when(s < 2)
                def _():
                    send_halo(n + 1, s)

            return add(parts, plane_sums(n + 1, s))

        send_sums(n + 1, lax.fori_loop(0, 3, renew, nothing))
        if n + 1 < STEPS:
            send_halo(n + 1, 2)

    def back(r, carry):
        for s in range(3):
            x = F[STEPS % 2, s, pl.ds(pl.multiple_of(NVT + r * 128, 8), 128), :]
            out[:, pl.ds(pl.multiple_of(s * PLANE + r * 128, 128), 128)] = x.T
        return carry

    lax.fori_loop(0, PLANE // 128, back, 0, unroll=3)
    S = wait_totals(STEPS)
    density, u, temp, heat = observables(S)
    for i, value in enumerate([density] + u + [temp] + heat):
        PR[i : i + 1] = value
    final = PR[0:8]
    for r in range(8):
        macro[:, r, :] = final[:, r * 16 : (r + 1) * 16]
    flows = jnp.concatenate([S[3], S[4], jnp.zeros((6, 128), F32)], axis=0)
    edges = weight * jnp.dot(
        flows, edge[:, 256:384], preferred_element_type=F32, precision=lax.Precision.HIGHEST
    )
    incident, upward, downward = edges[1:2, 0:8], edges[0:1, 8:16], edges[1:2, 8:16]
    flux[...] = jnp.where(
        gz == 0,
        jnp.where(bottom_code == 1, SAT_DENSITY * half_flux - incident, 0.0),
        jnp.where(top_code == 2, upward - downward, 0.0),
    )

    for n in range(STEPS):
        for s in range(3):

            @pl.when(row > 0)
            def _():
                radial_copy(n, s, 0).wait_send()

            @pl.when(row < last_row)
            def _():
                radial_copy(n, s, 1).wait_send()

            axial_copy(n, s).wait_send()
    for n in range(STEPS + 1):
        each_peer(lambda peer, k, n=n: sum_copy(n, vert, peer, k).wait_send())


def deliver(new, macro, flux, new_hbm, macro_hbm, flux_hbm, sems):
    copies = [
        pltpu.make_async_copy(src, dst, sems.at[k])
        for k, (src, dst) in enumerate([(new, new_hbm), (macro, macro_hbm), (flux, flux_hbm)])
    ]
    for copy in copies:
        copy.start()
    for copy in copies:
        copy.wait()


def solution(mesh):
    row_total, vert_total = mesh.shape["row"], mesh.shape["vert"]
    arrays, weight, half_flux = constants()

    def on_device(distribution, z_order, edge_codes):
        f = distribution.reshape(128, 3 * PLANE)
        outs = (
            jax.ShapeDtypeStruct((128, 3 * PLANE), F32),
            jax.ShapeDtypeStruct((8, 8, 16), F32),
            jax.ShapeDtypeStruct((1, 8), F32),
        )
        hbm = pl.BlockSpec(memory_space=pl.ANY)
        smem = pl.BlockSpec(memory_space=pltpu.SMEM)
        vmem = pl.BlockSpec(memory_space=pltpu.VMEM)
        dma = pltpu.SemaphoreType.DMA
        new, macro, flux = pl.pallas_call(
            functools.partial(kernel, (row_total, vert_total), weight, half_flux),
            out_shape=(pltpu.VMEM(outs[0].shape, F32), outs[1], outs[2]),
            in_specs=[hbm, smem, smem] + [hbm] * len(arrays),
            out_specs=(vmem, vmem, vmem),
            scratch_shapes=[
                pltpu.VMEM((3, 128, PLANE), F32),
                pltpu.VMEM((2, 3, PLANE + 2 * NVT, 128), F32),
                pltpu.VMEM((3, HALF, 128), F32),
                pltpu.VMEM((3, PLANE, 128), F32),
                pltpu.VMEM((3, PLANE, 256), F32),
                pltpu.VMEM((3, 2, 256, 256), BF16),
                pltpu.VMEM((3, NVT, 128), F32),
                pltpu.VMEM((3, NVT, 128), F32),
                pltpu.VMEM((3, 4, NVR, 128), F32),
                pltpu.VMEM((8, 128), F32),
            ]
            + [pltpu.VMEM(x.shape, x.dtype) for x in arrays]
            + [
                pltpu.VMEM((STEPS, 3, 2, 16, HALF), F32),
                pltpu.VMEM((STEPS, 3, 8, PLANE), F32),
                pltpu.VMEM((STEPS, 3, 2, 16, HALF), F32),
                pltpu.VMEM((STEPS, 3, 8, PLANE), F32),
                pltpu.VMEM((STEPS + 1, 16, 128), F32),
                pltpu.VMEM((STEPS + 1, vert_total, 16, 128), F32),
                dma((3,)),
                dma((len(arrays),)),
                dma((STEPS, 3, 2)),
                dma((STEPS, 3, 2)),
                dma((STEPS, 3)),
                dma((STEPS, 3)),
                dma((STEPS + 1, vert_total)),
                dma((STEPS + 1, vert_total)),
            ],
            compiler_params=pltpu.CompilerParams(
                collective_id=0, has_side_effects=True, vmem_limit_bytes=52 * 1024 * 1024
            ),
        )(f, z_order, edge_codes.reshape(2), *arrays)
        hold = lambda x: pltpu.with_memory_space_constraint(x, pltpu.VMEM)
        new, macro, flux = pl.pallas_call(
            deliver,
            out_shape=outs,
            in_specs=[vmem, vmem, vmem],
            out_specs=(hbm, hbm, hbm),
            scratch_shapes=[dma((3,))],
        )(hold(new), macro, flux)
        return new.reshape(distribution.shape), macro, flux

    in_specs = (P("row", "gz", "vert"), P("vert"), P(None, "row"))
    out_specs = (P("row", "gz", "vert"), P(None, "row", "gz"), P("gz", "row"))
    return jax.shard_map(
        on_device, mesh=mesh, in_specs=in_specs, out_specs=out_specs, check_vma=False
    )
```

```python
import functools
import math

import jax
import jax.numpy as jnp
import ml_dtypes
import numpy as np
from jax import lax
from jax.experimental import pallas as pl
from jax.experimental.pallas import tpu as pltpu
from jax.sharding import PartitionSpec as P

NODES = 8
NVR = 48
NVT = 48
NVZ = 48
STEPS = 2

ELEMENT_WIDTH = 4.0
TIME_STEP = 0.001
KNUDSEN = 0.005
VISCOUS_RATIO = 2.0 / 3.0
SAT_DENSITY = 1.5
SPEED_LIMIT = 5.0

PLANE = NVR * NVT
HALF = PLANE // 2
GRID_STEP = 2 * SPEED_LIMIT / NVR
UNIT = GRID_STEP / 2
MESH_IDS = pl.DeviceIdType.MESH
F32 = jnp.float32
BF16 = jnp.bfloat16


def legendre_pair(position, point_count):
    previous = 1.0
    current = position
    for degree in range(2, point_count + 1):
        previous, current = (
            current,
            ((2 * degree - 1) * position * current - (degree - 1) * previous) / degree,
        )
    slope = point_count * (position * current - previous) / (position * position - 1.0)
    return (current, slope)


def dg_tables(point_count):
    point_list = []
    weight_list = []
    for number in range(point_count):
        position = math.cos(math.pi * (number + 0.75) / (point_count + 0.5))
        for sweep in range(60):
            value, slope = legendre_pair(position, point_count)
            position = position - value / slope
        value, slope = legendre_pair(position, point_count)
        point_list.append(position)
        weight_list.append(2.0 / ((1.0 - position * position) * slope * slope))
    point_list = point_list[::-1]
    weight_list = weight_list[::-1]
    products = []
    for row_number in range(point_count):
        product_value = 1.0
        for other in range(point_count):
            if other != row_number:
                product_value = product_value * (point_list[row_number] - point_list[other])
        products.append(product_value)
    derivative_rows = []
    for row_number in range(point_count):
        entries = []
        for column in range(point_count):
            if column == row_number:
                total_value = 0.0
                for other in range(point_count):
                    if other != row_number:
                        total_value = total_value + 1.0 / (
                            point_list[row_number] - point_list[other]
                        )
                entries.append(total_value)
            else:
                entries.append(
                    products[row_number]
                    / products[column]
                    / (point_list[row_number] - point_list[column])
                )
        derivative_rows.append(entries)
    right_list = []
    left_list = []
    for column in range(point_count):
        right_value = 1.0
        left_value = 1.0
        for other in range(point_count):
            if other != column:
                right_value = right_value * (1.0 - point_list[other])
                left_value = left_value * (-1.0 - point_list[other])
        right_list.append(right_value / products[column])
        left_list.append(left_value / products[column])
    points = np.array(point_list)
    quad_weights = np.array(weight_list)
    derivative = np.array(derivative_rows)
    end_right = np.array(right_list)
    end_left = np.array(left_list)
    return (
        points,
        derivative,
        end_right / quad_weights,
        end_left / quad_weights,
        end_right,
        end_left,
    )


def speed_grid(point_count):
    return -SPEED_LIMIT + (np.arange(point_count) + 0.5) * (2.0 * SPEED_LIMIT / point_count)


def split_exact(values, count):
    parts = []
    rest = np.asarray(values, np.float64)
    for _ in range(count):
        head = rest.astype(ml_dtypes.bfloat16).astype(np.float64)
        parts.append(head)
        rest = rest - head
    assert not np.any(rest)
    return parts


def constants():
    points, derivative, lift_right, lift_left, end_right, end_left = dg_tables(NODES)
    eye8, eye16 = np.eye(8), np.eye(16)
    scale = -TIME_STEP * 2.0 / ELEMENT_WIDTH
    plus = derivative + np.outer(lift_left, end_left)
    minus = derivative - np.outer(lift_right, end_right)
    radial = np.zeros((3, 128, 256))
    for k, (core, ghost) in enumerate(
        [(minus, lift_right), (derivative, 0 * lift_right), (plus, -lift_left)]
    ):
        radial[k, :, :128] = np.kron(core, eye16)
        first = 160 if k == 2 else 128
        radial[k, :, first : first + 16] = np.kron(ghost[:, None], eye16)
    up = np.zeros((16, 16))
    up[:8, :8] = plus
    up[8:, 8:] = plus
    up[8:, :8] = -np.outer(lift_left, end_right)
    down = np.zeros((16, 16))
    down[:8, :8] = minus
    down[8:, 8:] = minus
    down[:8, 8:] = np.outer(lift_right, end_left)
    outflow = down.copy()
    outflow[8:, 8:] = derivative
    none = np.zeros(16)
    up_ghost = np.concatenate([-lift_left, np.zeros(8)])
    down_ghost = np.concatenate([np.zeros(8), lift_right])
    axial = np.zeros((5, 128, 160))
    for k, (core, ghost) in enumerate(
        [(up, none), (up, up_ghost), (down, down_ghost), (down, none), (outflow, none)]
    ):
        axial[k, :, :128] = np.kron(eye8, core)
        axial[k, :, 144:152] = np.kron(eye8, ghost[:, None])
    low_first = np.concatenate([end_left, np.zeros(8)])
    high_last = np.concatenate([np.zeros(8), end_right])
    trace = np.zeros((2, 2, 32, 128))
    for g, across in enumerate([high_last, low_first]):
        for h, along in enumerate([end_left, end_right]):
            trace[g, h, :16] = np.kron(along[None, :], eye16)
            trace[g, h, 16:24] = np.kron(eye8, across[None, :])
    odd = 2.0 * np.arange(48) + 1 - 48
    nr, nt = np.repeat(odd, 48), np.tile(odd, 48)
    square = nr * nr + nt * nt
    columns = (
        [np.ones(PLANE), nr, nt]
        + split_exact(nr * nr, 2)
        + split_exact(nt * nt, 2)
        + split_exact(nr * nt, 2)
        + split_exact(nr * square, 3)
        + split_exact(nt * square, 3)
        + [np.zeros(PLANE)]
    )
    basis = np.stack(columns)
    grid = speed_grid(48)
    column = np.ones((1, 128))
    index = np.arange(48)
    turn = TIME_STEP * grid / (2 * GRID_STEP)
    rows = np.stack(
        [
            grid[:, None] * column,
            np.exp(-(grid**2) / 2)[:, None] * column,
            (-turn * grid)[:, None] * column,
            (turn * (index < 47))[:, None] * column,
            (turn * (index > 0))[:, None] * column,
        ]
    )
    ones8 = np.ones(8)
    edge = np.zeros((128, 384))
    edge[:, :128] = np.kron(eye8, np.outer(low_first, np.ones(16)))
    edge[:, 128:256] = np.kron(eye8, np.outer(high_last, np.ones(16)))
    edge[:, 256:264] = np.kron(eye8, low_first[:, None])
    edge[:, 264:272] = np.kron(eye8, high_last[:, None])
    wall = np.zeros((8, 128))
    wall[0] = np.kron(ones8, np.concatenate([-scale * lift_left, np.zeros(8)]))
    wall[1] = np.kron(ones8, np.concatenate([np.zeros(8), scale * lift_right]))
    wall[2] = np.kron((1.0 + np.array(points)) / 2, np.ones(16))
    weight = GRID_STEP**3 / (2 * math.pi) ** 1.5
    half_flux = (
        weight
        * np.sum(np.exp(-(grid**2) / 2)) ** 2
        * np.sum(np.maximum(grid, 0.0) * np.exp(-(grid**2) / 2))
    )
    as_bf16 = lambda x: jnp.asarray(x.astype(np.float32).astype(ml_dtypes.bfloat16))
    as_f32 = lambda x: jnp.asarray(x.astype(np.float32))
    arrays = (
        as_bf16(scale * radial.transpose(0, 2, 1)),
        as_f32(scale * axial.transpose(0, 2, 1)),
        as_bf16(trace),
        as_bf16(basis),
        as_f32(rows),
        as_f32(edge),
        as_f32(wall),
    )
    return arrays, float(weight), float(half_flux)


def kernel(
    sizes, weight, half_flux,
    f_hbm, order, codes, radial_hbm, axial_hbm, trace_hbm, basis_hbm, rows_hbm, edge_hbm, wall_hbm,
    out, macro, flux,
    RAW, F, G, PART, TOUT, W, TURN, BYT, BYR, PR,
    radial, axial, trace, basis, rows, edge, wall,
    trR, trA, ghR, ghA, mine, ARB,
    load_sem, const_sem,
    rs_send, rs_recv, as_send, as_recv, ar_send, ar_recv,
):
    row_total, vert_total = sizes
    row, gz, vert = lax.axis_index("row"), lax.axis_index("gz"), lax.axis_index("vert")
    last_row = row_total - 1

    def load(s):
        lanes = pl.ds(pl.multiple_of(s * PLANE, 128), PLANE)
        return pltpu.make_async_copy(f_hbm.at[:, lanes], RAW.at[s], load_sem.at[s])

    consts = [
        pltpu.make_async_copy(src, dst, const_sem.at[k])
        for k, (src, dst) in enumerate(
            [
                (trace_hbm, trace),
                (basis_hbm, basis),
                (rows_hbm, rows),
                (radial_hbm, radial),
                (axial_hbm, axial),
                (edge_hbm, edge),
                (wall_hbm, wall),
            ]
        )
    ]
    load(0).start()
    for copy in consts[:2]:
        copy.start()
    load(1).start()
    load(2).start()
    for copy in consts[2:]:
        copy.start()

    barrier = pltpu.get_barrier_semaphore()

    def hello(k, carry):
        peer = lax.rem(vert + k, vert_total)
        pl.semaphore_signal(barrier, inc=1, device_id=(row, gz, peer), device_id_type=MESH_IDS)
        return carry

    lax.fori_loop(1, vert_total, hello, 0)
    pl.semaphore_signal(barrier, inc=1, device_id=(row, 1 - gz, vert), device_id_type=MESH_IDS)

    @pl.when(row > 0)
    def _():
        pl.semaphore_signal(barrier, inc=1, device_id=(row - 1, gz, vert), device_id_type=MESH_IDS)

    @pl.when(row < last_row)
    def _():
        pl.semaphore_signal(barrier, inc=1, device_id=(row + 1, gz, vert), device_id_type=MESH_IDS)

    speeds = [(2 * order[s] - (NVZ - 1)).astype(F32) * UNIT for s in range(3)]
    bottom_code, top_code = codes[0], codes[1]
    for n in range(STEPS):
        for s in range(3):
            F[n, s, 0:NVT] = jnp.zeros((NVT, 128), F32)
            F[n, s, NVT + PLANE :] = jnp.zeros((NVT, 128), F32)
    for s in range(3):
        G[s, :, 64:128] = jnp.zeros((HALF, 64), BF16)

    @pl.when(row == last_row)
    def _():
        for n in range(STEPS):
            for s in range(3):
                ghR[n, s, 0] = jnp.zeros((16, HALF), F32)


    def radial_copy(n, s, h):
        step = 1 if h else -1
        return pltpu.make_async_remote_copy(
            src_ref=trR.at[n, s, h],
            dst_ref=ghR.at[n, s, h],
            send_sem=rs_send.at[n, s, h],
            recv_sem=rs_recv.at[n, s, h],
            device_id=(row + step, gz, vert),
            device_id_type=MESH_IDS,
        )

    def axial_copy(n, s):
        return pltpu.make_async_remote_copy(
            src_ref=trA.at[n, s],
            dst_ref=ghA.at[n, s],
            send_sem=as_send.at[n, s],
            recv_sem=as_recv.at[n, s],
            device_id=(row, 1 - gz, vert),
            device_id_type=MESH_IDS,
        )

    def sum_copy(n, slot, peer, k):
        return pltpu.make_async_remote_copy(
            src_ref=mine.at[n],
            dst_ref=ARB.at[n, slot],
            send_sem=ar_send.at[n, k],
            recv_sem=ar_recv.at[n, slot],
            device_id=(row, gz, peer),
            device_id_type=MESH_IDS,
        )

    def each_peer(action):
        def body(k, carry):
            action(lax.rem(vert + k, vert_total), k)
            return carry

        lax.fori_loop(1, vert_total, body, 0, unroll=15)

    def send_halo(n, s):
        @pl.when(row > 0)
        def _():
            radial_copy(n, s, 0).start()

        @pl.when(row < last_row)
        def _():
            radial_copy(n, s, 1).start()

        axial_copy(n, s).start()

    over_lanes = (((1,), (1,)), ((), ()))

    def keep_traces(n, s, h, both):
        trR[n, s, h] = both[0:16]
        trA[n, s, :, h * HALF : (h + 1) * HALF] = both[16:24]

    def traces(n, s):
        for h in range(2):
            x = F[n % 2, s, NVT + h * HALF : NVT + (h + 1) * HALF, :].astype(BF16)
            both = lax.dot_general(trace[gz, h], x, over_lanes, preferred_element_type=F32)
            keep_traces(n, s, h, both)

    def plane_sums(n, s):
        total = jnp.zeros((16, 256), F32)
        for c in range(PLANE // 256):
            x = F[n % 2, s, NVT + c * 256 : NVT + (c + 1) * 256, :]
            hi = x.astype(BF16)
            lo = (x - hi.astype(F32)).astype(BF16)
            total += jnp.dot(
                basis[:, c * 256 : (c + 1) * 256],
                jnp.concatenate([hi, lo], axis=1),
                preferred_element_type=F32,
            )
        return combine(s, total)

    def ghosts(n, s):
        @pl.when(row < last_row)
        def _():
            radial_copy(n, s, 0).wait_recv()

        @pl.when(row > 0)
        def _():
            radial_copy(n, s, 1).wait_recv()

        @pl.when(row == 0)
        def _():
            own = trR[n, s, 0]
            ghR[n, s, 1] = jnp.concatenate(
                [own[:, k * NVT : (k + 1) * NVT] for k in reversed(range(NVR // 2))], axis=1
            )

        axial_copy(n, s).wait_recv()
        spare = jnp.zeros((8, 128), F32)

        def turn(k, carry):
            low = pl.ds(pl.multiple_of(k * 128, 128), 128)
            high = pl.ds(pl.multiple_of(HALF + k * 128, 128), 128)
            table = [ghR[n, s, 0, :, low], ghA[n, s, :, low], spare]
            table += [ghR[n, s, 1, :, low], ghA[n, s, :, high], spare]
            G[s, low, 0:64] = jnp.concatenate(table, axis=0).T.astype(BF16)
            return carry

        lax.fori_loop(0, HALF // 128, turn, 0, unroll=9)

    def combine(s, total):
        table = total[:, 0:128] + total[:, 128:256]
        z = (2 * order[s] - (NVZ - 1)).astype(F32) * UNIT
        g = [table[i : i + 1] for i in range(15)]
        b0, br, bt = g[0], UNIT * g[1], UNIT * g[2]
        brr, btt, brt = (UNIT**2 * (g[i] + g[i + 1]) for i in (3, 5, 7))
        br3, bt3 = (UNIT**3 * (g[i] + (g[i + 1] + g[i + 2])) for i in (9, 12))
        return [
            b0,
            br,
            bt,
            jnp.maximum(z, 0.0) * b0,
            jnp.maximum(-z, 0.0) * b0,
            brr,
            btt,
            z * z * b0,
            brt,
            z * br,
            z * bt,
            br3 + z * z * br,
            bt3 + z * z * bt,
            z * (brr + btt) + (z * z * z) * b0,
        ]

    def send_sums(n, parts):
        for i in range(14):
            mine[n, i : i + 1] = parts[i]
        mine[n, 14:16] = jnp.zeros((2, 128), F32)
        ARB[n, vert] = mine[n]
        each_peer(lambda peer, k: sum_copy(n, vert, peer, k).start())

    def wait_totals(n):
        each_peer(lambda peer, k: sum_copy(n, peer, peer, k).wait_recv())
        terms = [ARB[n, k] for k in range(vert_total)]
        while len(terms) > 1:
            terms = [terms[i] + terms[i + 1] for i in range(0, len(terms), 2)]
        return [terms[0][i : i + 1] for i in range(14)]

    def observables(S):
        m = S
        inv = 1.0 / m[0]
        u = [m[1] * inv, m[2] * inv, (m[3] - m[4]) * inv]
        usq = u[0] * u[0] + u[1] * u[1] + u[2] * u[2]
        tr = m[5] + m[6] + m[7]
        temp = (tr * inv - usq) / 3.0
        tensor = [[m[5], m[8], m[9]], [m[8], m[6], m[10]], [m[9], m[10], m[7]]]
        heat = []
        for i in range(3):
            mixed = tensor[i][0] * u[0] + tensor[i][1] * u[1] + tensor[i][2] * u[2]
            raw = m[11 + i] - 2.0 * mixed - u[i] * tr + (2.0 * usq * m[0]) * u[i]
            heat.append((0.5 * weight) * raw)
        return weight * m[0], u, temp, heat

    def params(S):
        density, u, temp, heat = observables(S)
        flows = jnp.concatenate([S[3], S[4], jnp.zeros((6, 128), F32)], axis=0)
        edges = jnp.dot(
            flows, edge[:, 0:256], preferred_element_type=F32, precision=lax.Precision.HIGHEST
        )
        incident = weight * edges[1:2, 0:128]
        upward = weight * edges[0:1, 128:256]
        bottom = jnp.where(bottom_code == 1, SAT_DENSITY, incident / half_flux)
        top = jnp.where(top_code == 2, 0.0, upward / half_flux)
        wall_gain = jnp.where(gz == 0, bottom * wall[0:1], top * wall[1:2])
        inv_temp = 1.0 / temp
        kappa = ((1.0 - VISCOUS_RATIO) / 5.0) * inv_temp * inv_temp / density
        rate = (TIME_STEP / KNUDSEN) * density
        peak = rate * density * inv_temp * lax.rsqrt(temp)
        PR[0:1] = 1.0 - rate
        centred = rows[0] - u[0]
        square = centred * centred
        around = [
            jnp.exp(square * (-0.5 * inv_temp)),
            centred * (kappa * heat[0]),
            square * inv_temp - 5.0,
        ]
        centred = rows[0] - u[1]
        square = centred * centred
        BYT[0] = jnp.exp(square * (-0.5 * inv_temp))
        BYT[1] = centred * (kappa * heat[1])
        BYT[2] = square * inv_temp
        for s in range(3):
            z = speeds[s]
            cz = z - u[2]
            inward = jnp.where(gz == 0, jnp.maximum(z, 0.0), jnp.minimum(z, 0.0))
            BYR[s, 0] = around[0] * (peak * jnp.exp(-0.5 * cz * cz * inv_temp))
            BYR[s, 1] = around[1] + kappa * heat[2] * cz
            BYR[s, 2] = around[2] + cz * cz * inv_temp
            BYR[s, 3] = rows[1] * (
                inward * wall_gain * jnp.exp(jnp.zeros((1, 128), F32) - 0.5 * z * z)
            )

    for copy in consts[:2]:
        copy.wait()
    nothing = tuple(jnp.zeros((1, 128), F32) for _ in range(14))

    def add(parts, more):
        return tuple(a + b for a, b in zip(parts, more))

    def begin(s, parts):
        load(s).wait()
        for h in range(2):
            lanes = slice(h * HALF, (h + 1) * HALF)
            keep_traces(0, s, h, jnp.dot(
                trace[gz, h], RAW[s, :, lanes].astype(BF16), preferred_element_type=F32
            ))

        @pl.when(s == 0)
        def _():
            peers = vert_total + (row > 0).astype(jnp.int32) + (row < last_row).astype(jnp.int32)
            pl.semaphore_wait(barrier, peers)

        @pl.when(s < 2)
        def _():
            send_halo(0, s)

        def split(r, carry):
            at = pl.ds(pl.multiple_of(r * 128, 128), 128)
            F[0, s, pl.ds(pl.multiple_of(NVT + r * 128, 8), 128), :] = RAW[s, :, at].T
            return carry

        lax.fori_loop(0, PLANE // 128, split, 0, unroll=9)
        return add(parts, plane_sums(0, s))

    send_sums(0, lax.fori_loop(0, 3, begin, nothing))
    send_halo(0, 2)

    for copy in consts[2:]:
        copy.wait()
    for s in range(3):
        z = speeds[s]
        up = jnp.where(gz == 0, axial[0], axial[1])
        down = jnp.where(gz == 0, axial[2], jnp.where(top_code == 2, axial[4], axial[3]))
        along = (z * jnp.where(z > 0, up, down)).astype(BF16)
        for h in range(2):
            W[s, h, 0:128, 128:256] = along[0:128]
            W[s, h, 128:256, 128:256] = jnp.zeros((128, 128), BF16)
            W[s, h, 128 + 32 * h : 160 + 32 * h, 128:256] = along[128:160]
        W[s, 0, :, 0:128] = radial[jnp.where(row == last_row, 1, 0)]
        W[s, 1, :, 0:128] = radial[2]

    inverse = 1.0 / ((row.astype(F32) + wall[2:3]) * ELEMENT_WIDTH)
    for k in range(3):
        TURN[k] = rows[2 + k] * inverse

    for n in range(STEPS):
        def move(s, none, n=n):
            ghosts(n, s)

            for h in range(2):
                x = F[n, s, NVT + h * HALF : NVT + (h + 1) * HALF, :].astype(BF16)
                operand = jnp.concatenate([x, G[s]], axis=1)
                TOUT[s, pl.ds(h * HALF, HALF), :] = jnp.dot(
                    operand, W[s, h], preferred_element_type=F32
                )

            def stream(a, carry):
                at = pl.ds(pl.multiple_of(a * NVT, 16), NVT)
                behind, ahead = (
                    F[n, s, pl.ds(pl.multiple_of((a + k) * NVT, 8), NVT), :] for k in (0, 2)
                )
                speed = (2 * a - (NVR - 1)).astype(F32) * UNIT
                base = (a + 1) * NVT
                around = (
                    TURN[1] * F[n, s, pl.ds(base + 1, NVT), :]
                    - TURN[2] * F[n, s, pl.ds(base - 1, NVT), :]
                )
                PART[s, at, :] = (
                    TURN[0] * (ahead - behind)
                    + speed * (around + TOUT[s, at, 0:128])
                    + TOUT[s, at, 128:256]
                )
                return carry

            lax.fori_loop(0, NVR, stream, 0, unroll=16)
            return none

        lax.fori_loop(0, 3, move, 0)
        params(wait_totals(n))

        def renew(s, parts, n=n):
            def update(a, carry):
                at = pl.ds(pl.multiple_of(a * NVT, 16), NVT)
                own = pl.ds(pl.multiple_of((a + 1) * NVT, 8), NVT)
                peak, heat, excess, wall_row = (BYR[s, k, pl.ds(a, 1), :] for k in range(4))
                goal = (BYT[0] * peak) * (1.0 + (BYT[1] + heat) * (BYT[2] + excess))
                F[(n + 1) % 2, s, own, :] = (
                    PR[0:1] * F[n, s, own, :] + PART[s, at, :] + wall_row * rows[1] + goal
                )
                return carry

            lax.fori_loop(0, NVR, update, 0, unroll=16)
            if n + 1 < STEPS:
                traces(n + 1, s)

                @pl.when(s < 2)
                def _():
                    send_halo(n + 1, s)

            return add(parts, plane_sums(n + 1, s))

        send_sums(n + 1, lax.fori_loop(0, 3, renew, nothing))
        if n + 1 < STEPS:
            send_halo(n + 1, 2)

    def back(r, carry):
        for s in range(3):
            x = F[STEPS % 2, s, pl.ds(pl.multiple_of(NVT + r * 128, 8), 128), :]
            out[:, pl.ds(pl.multiple_of(s * PLANE + r * 128, 128), 128)] = x.T
        return carry

    lax.fori_loop(0, PLANE // 128, back, 0, unroll=3)
    S = wait_totals(STEPS)
    density, u, temp, heat = observables(S)
    for i, value in enumerate([density] + u + [temp] + heat):
        PR[i : i + 1] = value
    final = PR[0:8]
    for r in range(8):
        macro[:, r, :] = final[:, r * 16 : (r + 1) * 16]
    flows = jnp.concatenate([S[3], S[4], jnp.zeros((6, 128), F32)], axis=0)
    edges = weight * jnp.dot(
        flows, edge[:, 256:384], preferred_element_type=F32, precision=lax.Precision.HIGHEST
    )
    incident, upward, downward = edges[1:2, 0:8], edges[0:1, 8:16], edges[1:2, 8:16]
    flux[...] = jnp.where(
        gz == 0,
        jnp.where(bottom_code == 1, SAT_DENSITY * half_flux - incident, 0.0),
        jnp.where(top_code == 2, upward - downward, 0.0),
    )

    for n in range(STEPS):
        for s in range(3):

            @pl.when(row > 0)
            def _():
                radial_copy(n, s, 0).wait_send()

            @pl.when(row < last_row)
            def _():
                radial_copy(n, s, 1).wait_send()

            axial_copy(n, s).wait_send()
    for n in range(STEPS + 1):
        each_peer(lambda peer, k, n=n: sum_copy(n, vert, peer, k).wait_send())


def deliver(new, macro, flux, new_hbm, macro_hbm, flux_hbm, sems):
    copies = [
        pltpu.make_async_copy(src, dst, sems.at[k])
        for k, (src, dst) in enumerate([(new, new_hbm), (macro, macro_hbm), (flux, flux_hbm)])
    ]
    for copy in copies:
        copy.start()
    for copy in copies:
        copy.wait()


def solution(mesh):
    row_total, vert_total = mesh.shape["row"], mesh.shape["vert"]
    arrays, weight, half_flux = constants()

    def on_device(distribution, z_order, edge_codes):
        f = distribution.reshape(128, 3 * PLANE)
        outs = (
            jax.ShapeDtypeStruct((128, 3 * PLANE), F32),
            jax.ShapeDtypeStruct((8, 8, 16), F32),
            jax.ShapeDtypeStruct((1, 8), F32),
        )
        hbm = pl.BlockSpec(memory_space=pl.ANY)
        smem = pl.BlockSpec(memory_space=pltpu.SMEM)
        vmem = pl.BlockSpec(memory_space=pltpu.VMEM)
        dma = pltpu.SemaphoreType.DMA
        new, macro, flux = pl.pallas_call(
            functools.partial(kernel, (row_total, vert_total), weight, half_flux),
            out_shape=(pltpu.VMEM(outs[0].shape, F32), outs[1], outs[2]),
            in_specs=[hbm, smem, smem] + [hbm] * len(arrays),
            out_specs=(vmem, vmem, vmem),
            scratch_shapes=[
                pltpu.VMEM((3, 128, PLANE), F32),
                pltpu.VMEM((2, 3, PLANE + 2 * NVT, 128), F32),
                pltpu.VMEM((3, HALF, 128), BF16),
                pltpu.VMEM((3, PLANE, 128), F32),
                pltpu.VMEM((3, PLANE, 256), F32),
                pltpu.VMEM((3, 2, 256, 256), BF16),
                pltpu.VMEM((3, NVT, 128), F32),
                pltpu.VMEM((3, NVT, 128), F32),
                pltpu.VMEM((3, 4, NVR, 128), F32),
                pltpu.VMEM((8, 128), F32),
            ]
            + [pltpu.VMEM(x.shape, x.dtype) for x in arrays]
            + [
                pltpu.VMEM((STEPS, 3, 2, 16, HALF), F32),
                pltpu.VMEM((STEPS, 3, 8, PLANE), F32),
                pltpu.VMEM((STEPS, 3, 2, 16, HALF), F32),
                pltpu.VMEM((STEPS, 3, 8, PLANE), F32),
                pltpu.VMEM((STEPS + 1, 16, 128), F32),
                pltpu.VMEM((STEPS + 1, vert_total, 16, 128), F32),
                dma((3,)),
                dma((len(arrays),)),
                dma((STEPS, 3, 2)),
                dma((STEPS, 3, 2)),
                dma((STEPS, 3)),
                dma((STEPS, 3)),
                dma((STEPS + 1, vert_total)),
                dma((STEPS + 1, vert_total)),
            ],
            compiler_params=pltpu.CompilerParams(
                collective_id=0, has_side_effects=True, vmem_limit_bytes=52 * 1024 * 1024
            ),
        )(f, z_order, edge_codes.reshape(2), *arrays)
        hold = lambda x: pltpu.with_memory_space_constraint(x, pltpu.VMEM)
        new, macro, flux = pl.pallas_call(
            deliver,
            out_shape=outs,
            in_specs=[vmem, vmem, vmem],
            out_specs=(hbm, hbm, hbm),
            scratch_shapes=[dma((3,))],
        )(hold(new), macro, flux)
        return new.reshape(distribution.shape), macro, flux

    in_specs = (P("row", "gz", "vert"), P("vert"), P(None, "row"))
    out_specs = (P("row", "gz", "vert"), P(None, "row", "gz"), P("gz", "row"))
    return jax.shard_map(
        on_device, mesh=mesh, in_specs=in_specs, out_specs=out_specs, check_vma=False
    )
```

```python
import functools
import math

import jax
import jax.numpy as jnp
import ml_dtypes
import numpy as np
from jax import lax
from jax.experimental import pallas as pl
from jax.experimental.pallas import tpu as pltpu
from jax.sharding import PartitionSpec as P

NODES = 8
NVR = 48
NVT = 48
NVZ = 48
STEPS = 2

ELEMENT_WIDTH = 4.0
TIME_STEP = 0.001
KNUDSEN = 0.005
VISCOUS_RATIO = 2.0 / 3.0
SAT_DENSITY = 1.5
SPEED_LIMIT = 5.0

PLANE = NVR * NVT
HALF = PLANE // 2
GRID_STEP = 2 * SPEED_LIMIT / NVR
UNIT = GRID_STEP / 2
MESH_IDS = pl.DeviceIdType.MESH
F32 = jnp.float32
BF16 = jnp.bfloat16


def legendre_pair(position, point_count):
    previous = 1.0
    current = position
    for degree in range(2, point_count + 1):
        previous, current = (
            current,
            ((2 * degree - 1) * position * current - (degree - 1) * previous) / degree,
        )
    slope = point_count * (position * current - previous) / (position * position - 1.0)
    return (current, slope)


def dg_tables(point_count):
    point_list = []
    weight_list = []
    for number in range(point_count):
        position = math.cos(math.pi * (number + 0.75) / (point_count + 0.5))
        for sweep in range(60):
            value, slope = legendre_pair(position, point_count)
            position = position - value / slope
        value, slope = legendre_pair(position, point_count)
        point_list.append(position)
        weight_list.append(2.0 / ((1.0 - position * position) * slope * slope))
    point_list = point_list[::-1]
    weight_list = weight_list[::-1]
    products = []
    for row_number in range(point_count):
        product_value = 1.0
        for other in range(point_count):
            if other != row_number:
                product_value = product_value * (point_list[row_number] - point_list[other])
        products.append(product_value)
    derivative_rows = []
    for row_number in range(point_count):
        entries = []
        for column in range(point_count):
            if column == row_number:
                total_value = 0.0
                for other in range(point_count):
                    if other != row_number:
                        total_value = total_value + 1.0 / (
                            point_list[row_number] - point_list[other]
                        )
                entries.append(total_value)
            else:
                entries.append(
                    products[row_number]
                    / products[column]
                    / (point_list[row_number] - point_list[column])
                )
        derivative_rows.append(entries)
    right_list = []
    left_list = []
    for column in range(point_count):
        right_value = 1.0
        left_value = 1.0
        for other in range(point_count):
            if other != column:
                right_value = right_value * (1.0 - point_list[other])
                left_value = left_value * (-1.0 - point_list[other])
        right_list.append(right_value / products[column])
        left_list.append(left_value / products[column])
    points = np.array(point_list)
    quad_weights = np.array(weight_list)
    derivative = np.array(derivative_rows)
    end_right = np.array(right_list)
    end_left = np.array(left_list)
    return (
        points,
        derivative,
        end_right / quad_weights,
        end_left / quad_weights,
        end_right,
        end_left,
    )


def speed_grid(point_count):
    return -SPEED_LIMIT + (np.arange(point_count) + 0.5) * (2.0 * SPEED_LIMIT / point_count)


def split_exact(values, count):
    parts = []
    rest = np.asarray(values, np.float64)
    for _ in range(count):
        head = rest.astype(ml_dtypes.bfloat16).astype(np.float64)
        parts.append(head)
        rest = rest - head
    assert not np.any(rest)
    return parts


def constants():
    points, derivative, lift_right, lift_left, end_right, end_left = dg_tables(NODES)
    eye8, eye16 = np.eye(8), np.eye(16)
    scale = -TIME_STEP * 2.0 / ELEMENT_WIDTH
    plus = derivative + np.outer(lift_left, end_left)
    minus = derivative - np.outer(lift_right, end_right)
    radial = np.zeros((3, 128, 256))
    for k, (core, ghost) in enumerate(
        [(minus, lift_right), (derivative, 0 * lift_right), (plus, -lift_left)]
    ):
        radial[k, :, :128] = np.kron(core, eye16)
        first = 160 if k == 2 else 128
        radial[k, :, first : first + 16] = np.kron(ghost[:, None], eye16)
    up = np.zeros((16, 16))
    up[:8, :8] = plus
    up[8:, 8:] = plus
    up[8:, :8] = -np.outer(lift_left, end_right)
    down = np.zeros((16, 16))
    down[:8, :8] = minus
    down[8:, 8:] = minus
    down[:8, 8:] = np.outer(lift_right, end_left)
    outflow = down.copy()
    outflow[8:, 8:] = derivative
    none = np.zeros(16)
    up_ghost = np.concatenate([-lift_left, np.zeros(8)])
    down_ghost = np.concatenate([np.zeros(8), lift_right])
    axial = np.zeros((5, 128, 160))
    for k, (core, ghost) in enumerate(
        [(up, none), (up, up_ghost), (down, down_ghost), (down, none), (outflow, none)]
    ):
        axial[k, :, :128] = np.kron(eye8, core)
        axial[k, :, 144:152] = np.kron(eye8, ghost[:, None])
    low_first = np.concatenate([end_left, np.zeros(8)])
    high_last = np.concatenate([np.zeros(8), end_right])
    trace = np.zeros((2, 2, 32, 128))
    for g, across in enumerate([high_last, low_first]):
        for h, along in enumerate([end_left, end_right]):
            trace[g, h, :16] = np.kron(along[None, :], eye16)
            trace[g, h, 16:24] = np.kron(eye8, across[None, :])
    odd = 2.0 * np.arange(48) + 1 - 48
    nr, nt = np.repeat(odd, 48), np.tile(odd, 48)
    square = nr * nr + nt * nt
    columns = (
        [np.ones(PLANE), nr, nt]
        + split_exact(nr * nr, 2)
        + split_exact(nt * nt, 2)
        + split_exact(nr * nt, 2)
        + split_exact(nr * square, 3)
        + split_exact(nt * square, 3)
        + [np.zeros(PLANE)]
    )
    basis = np.stack(columns)
    grid = speed_grid(48)
    column = np.ones((1, 128))
    index = np.arange(48)
    turn = TIME_STEP * grid / (2 * GRID_STEP)
    rows = np.stack(
        [
            grid[:, None] * column,
            np.exp(-(grid**2) / 2)[:, None] * column,
            (-turn * grid)[:, None] * column,
            (turn * (index < 47))[:, None] * column,
            (turn * (index > 0))[:, None] * column,
        ]
    )
    ones8 = np.ones(8)
    edge = np.zeros((128, 384))
    edge[:, :128] = np.kron(eye8, np.outer(low_first, np.ones(16)))
    edge[:, 128:256] = np.kron(eye8, np.outer(high_last, np.ones(16)))
    edge[:, 256:264] = np.kron(eye8, low_first[:, None])
    edge[:, 264:272] = np.kron(eye8, high_last[:, None])
    wall = np.zeros((8, 128))
    wall[0] = np.kron(ones8, np.concatenate([-scale * lift_left, np.zeros(8)]))
    wall[1] = np.kron(ones8, np.concatenate([np.zeros(8), scale * lift_right]))
    wall[2] = np.kron((1.0 + np.array(points)) / 2, np.ones(16))
    weight = GRID_STEP**3 / (2 * math.pi) ** 1.5
    half_flux = (
        weight
        * np.sum(np.exp(-(grid**2) / 2)) ** 2
        * np.sum(np.maximum(grid, 0.0) * np.exp(-(grid**2) / 2))
    )
    as_bf16 = lambda x: jnp.asarray(x.astype(np.float32).astype(ml_dtypes.bfloat16))
    as_f32 = lambda x: jnp.asarray(x.astype(np.float32))
    arrays = (
        as_bf16(scale * radial.transpose(0, 2, 1)),
        as_f32(scale * axial.transpose(0, 2, 1)),
        as_bf16(trace),
        as_bf16(basis),
        as_f32(rows),
        as_f32(edge),
        as_f32(wall),
    )
    return arrays, float(weight), float(half_flux)


def kernel(
    sizes, weight, half_flux,
    f_hbm, order, codes, radial_hbm, axial_hbm, trace_hbm, basis_hbm, rows_hbm, edge_hbm, wall_hbm,
    out, macro, flux,
    RAW, F, G, PART, TOUT, W, TURN, BYT, BYR, PR,
    radial, axial, trace, basis, rows, edge, wall,
    trR, trA, ghR, ghA, mine, ARB,
    load_sem, const_sem,
    rs_send, rs_recv, as_send, as_recv, ar_send, ar_recv,
):
    row_total, vert_total = sizes
    row, gz, vert = lax.axis_index("row"), lax.axis_index("gz"), lax.axis_index("vert")
    last_row = row_total - 1

    def load(s):
        lanes = pl.ds(pl.multiple_of(s * PLANE, 128), PLANE)
        return pltpu.make_async_copy(f_hbm.at[:, lanes], RAW.at[s], load_sem.at[s])

    consts = [
        pltpu.make_async_copy(src, dst, const_sem.at[k])
        for k, (src, dst) in enumerate(
            [
                (trace_hbm, trace),
                (basis_hbm, basis),
                (rows_hbm, rows),
                (radial_hbm, radial),
                (axial_hbm, axial),
                (edge_hbm, edge),
                (wall_hbm, wall),
            ]
        )
    ]
    load(0).start()
    for copy in consts[:2]:
        copy.start()
    load(1).start()
    load(2).start()
    for copy in consts[2:]:
        copy.start()

    barrier = pltpu.get_barrier_semaphore()

    def hello(k, carry):
        peer = lax.rem(vert + k, vert_total)
        pl.semaphore_signal(barrier, inc=1, device_id=(row, gz, peer), device_id_type=MESH_IDS)
        return carry

    lax.fori_loop(1, vert_total, hello, 0)
    pl.semaphore_signal(barrier, inc=1, device_id=(row, 1 - gz, vert), device_id_type=MESH_IDS)

    @pl.when(row > 0)
    def _():
        pl.semaphore_signal(barrier, inc=1, device_id=(row - 1, gz, vert), device_id_type=MESH_IDS)

    @pl.when(row < last_row)
    def _():
        pl.semaphore_signal(barrier, inc=1, device_id=(row + 1, gz, vert), device_id_type=MESH_IDS)

    speeds = [(2 * order[s] - (NVZ - 1)).astype(F32) * UNIT for s in range(3)]
    bottom_code, top_code = codes[0], codes[1]
    for n in range(STEPS):
        for s in range(3):
            F[n, s, 0:NVT] = jnp.zeros((NVT, 128), F32)
            F[n, s, NVT + PLANE :] = jnp.zeros((NVT, 128), F32)
    for s in range(3):
        G[s, :, 64:128] = jnp.zeros((HALF, 64), BF16)

    @pl.when(row == last_row)
    def _():
        for n in range(STEPS):
            for s in range(3):
                ghR[n, s, 0] = jnp.zeros((16, HALF), F32)


    def radial_copy(n, s, h):
        step = 1 if h else -1
        return pltpu.make_async_remote_copy(
            src_ref=trR.at[n, s, h],
            dst_ref=ghR.at[n, s, h],
            send_sem=rs_send.at[n, s, h],
            recv_sem=rs_recv.at[n, s, h],
            device_id=(row + step, gz, vert),
            device_id_type=MESH_IDS,
        )

    def axial_copy(n, s):
        return pltpu.make_async_remote_copy(
            src_ref=trA.at[n, s],
            dst_ref=ghA.at[n, s],
            send_sem=as_send.at[n, s],
            recv_sem=as_recv.at[n, s],
            device_id=(row, 1 - gz, vert),
            device_id_type=MESH_IDS,
        )

    def sum_copy(n, slot, peer, k):
        return pltpu.make_async_remote_copy(
            src_ref=mine.at[n],
            dst_ref=ARB.at[n, slot],
            send_sem=ar_send.at[n, k],
            recv_sem=ar_recv.at[n, slot],
            device_id=(row, gz, peer),
            device_id_type=MESH_IDS,
        )

    def each_peer(action):
        def body(k, carry):
            action(lax.rem(vert + k, vert_total), k)
            return carry

        lax.fori_loop(1, vert_total, body, 0, unroll=15)

    def send_halo(n, s):
        @pl.when(row > 0)
        def _():
            radial_copy(n, s, 0).start()

        @pl.when(row < last_row)
        def _():
            radial_copy(n, s, 1).start()

        axial_copy(n, s).start()

    over_lanes = (((1,), (1,)), ((), ()))

    def keep_traces(n, s, h, both):
        trR[n, s, h] = both[0:16]
        trA[n, s, :, h * HALF : (h + 1) * HALF] = both[16:24]

    def traces(n, s):
        for h in range(2):
            x = F[n % 2, s, NVT + h * HALF : NVT + (h + 1) * HALF, :].astype(BF16)
            both = lax.dot_general(x, trace[gz, h], over_lanes, preferred_element_type=F32)
            keep_traces(n, s, h, both.T)

    def plane_sums(n, s):
        total = jnp.zeros((16, 256), F32)
        for c in range(PLANE // 256):
            x = F[n % 2, s, NVT + c * 256 : NVT + (c + 1) * 256, :]
            hi = x.astype(BF16)
            lo = (x - hi.astype(F32)).astype(BF16)
            total += jnp.dot(
                basis[:, c * 256 : (c + 1) * 256],
                jnp.concatenate([hi, lo], axis=1),
                preferred_element_type=F32,
            )
        return combine(s, total)

    def ghosts(n, s):
        @pl.when(row < last_row)
        def _():
            radial_copy(n, s, 0).wait_recv()

        @pl.when(row > 0)
        def _():
            radial_copy(n, s, 1).wait_recv()

        @pl.when(row == 0)
        def _():
            own = trR[n, s, 0]
            ghR[n, s, 1] = jnp.concatenate(
                [own[:, k * NVT : (k + 1) * NVT] for k in reversed(range(NVR // 2))], axis=1
            )

        axial_copy(n, s).wait_recv()
        spare = jnp.zeros((8, 128), F32)

        def turn(k, carry):
            low = pl.ds(pl.multiple_of(k * 128, 128), 128)
            high = pl.ds(pl.multiple_of(HALF + k * 128, 128), 128)
            table = [ghR[n, s, 0, :, low], ghA[n, s, :, low], spare]
            table += [ghR[n, s, 1, :, low], ghA[n, s, :, high], spare]
            G[s, low, 0:64] = jnp.concatenate(table, axis=0).T.astype(BF16)
            return carry

        lax.fori_loop(0, HALF // 128, turn, 0, unroll=9)

    def combine(s, total):
        table = total[:, 0:128] + total[:, 128:256]
        z = (2 * order[s] - (NVZ - 1)).astype(F32) * UNIT
        g = [table[i : i + 1] for i in range(15)]
        b0, br, bt = g[0], UNIT * g[1], UNIT * g[2]
        brr, btt, brt = (UNIT**2 * (g[i] + g[i + 1]) for i in (3, 5, 7))
        br3, bt3 = (UNIT**3 * (g[i] + (g[i + 1] + g[i + 2])) for i in (9, 12))
        return [
            b0,
            br,
            bt,
            jnp.maximum(z, 0.0) * b0,
            jnp.maximum(-z, 0.0) * b0,
            brr,
            btt,
            z * z * b0,
            brt,
            z * br,
            z * bt,
            br3 + z * z * br,
            bt3 + z * z * bt,
            z * (brr + btt) + (z * z * z) * b0,
        ]

    def send_sums(n, parts):
        for i in range(14):
            mine[n, i : i + 1] = parts[i]
        mine[n, 14:16] = jnp.zeros((2, 128), F32)
        ARB[n, vert] = mine[n]
        each_peer(lambda peer, k: sum_copy(n, vert, peer, k).start())

    def wait_totals(n):
        each_peer(lambda peer, k: sum_copy(n, peer, peer, k).wait_recv())
        terms = [ARB[n, k] for k in range(vert_total)]
        while len(terms) > 1:
            terms = [terms[i] + terms[i + 1] for i in range(0, len(terms), 2)]
        return [terms[0][i : i + 1] for i in range(14)]

    def observables(S):
        m = S
        inv = 1.0 / m[0]
        u = [m[1] * inv, m[2] * inv, (m[3] - m[4]) * inv]
        usq = u[0] * u[0] + u[1] * u[1] + u[2] * u[2]
        tr = m[5] + m[6] + m[7]
        temp = (tr * inv - usq) / 3.0
        tensor = [[m[5], m[8], m[9]], [m[8], m[6], m[10]], [m[9], m[10], m[7]]]
        heat = []
        for i in range(3):
            mixed = tensor[i][0] * u[0] + tensor[i][1] * u[1] + tensor[i][2] * u[2]
            raw = m[11 + i] - 2.0 * mixed - u[i] * tr + (2.0 * usq * m[0]) * u[i]
            heat.append((0.5 * weight) * raw)
        return weight * m[0], u, temp, heat

    def params(S):
        density, u, temp, heat = observables(S)
        flows = jnp.concatenate([S[3], S[4], jnp.zeros((6, 128), F32)], axis=0)
        edges = jnp.dot(
            flows, edge[:, 0:256], preferred_element_type=F32, precision=lax.Precision.HIGHEST
        )
        incident = weight * edges[1:2, 0:128]
        upward = weight * edges[0:1, 128:256]
        bottom = jnp.where(bottom_code == 1, SAT_DENSITY, incident / half_flux)
        top = jnp.where(top_code == 2, 0.0, upward / half_flux)
        wall_gain = jnp.where(gz == 0, bottom * wall[0:1], top * wall[1:2])
        inv_temp = 1.0 / temp
        kappa = ((1.0 - VISCOUS_RATIO) / 5.0) * inv_temp * inv_temp / density
        rate = (TIME_STEP / KNUDSEN) * density
        peak = rate * density * inv_temp * lax.rsqrt(temp)
        PR[0:1] = 1.0 - rate
        centred = rows[0] - u[0]
        square = centred * centred
        around = [
            jnp.exp(square * (-0.5 * inv_temp)),
            centred * (kappa * heat[0]),
            square * inv_temp - 5.0,
        ]
        centred = rows[0] - u[1]
        square = centred * centred
        BYT[0] = jnp.exp(square * (-0.5 * inv_temp))
        BYT[1] = centred * (kappa * heat[1])
        BYT[2] = square * inv_temp
        for s in range(3):
            z = speeds[s]
            cz = z - u[2]
            inward = jnp.where(gz == 0, jnp.maximum(z, 0.0), jnp.minimum(z, 0.0))
            BYR[s, 0] = around[0] * (peak * jnp.exp(-0.5 * cz * cz * inv_temp))
            BYR[s, 1] = around[1] + kappa * heat[2] * cz
            BYR[s, 2] = around[2] + cz * cz * inv_temp
            BYR[s, 3] = rows[1] * (
                inward * wall_gain * jnp.exp(jnp.zeros((1, 128), F32) - 0.5 * z * z)
            )

    for copy in consts[:2]:
        copy.wait()
    nothing = tuple(jnp.zeros((1, 128), F32) for _ in range(14))

    def add(parts, more):
        return tuple(a + b for a, b in zip(parts, more))

    def begin(s, parts):
        load(s).wait()
        for h in range(2):
            lanes = slice(h * HALF, (h + 1) * HALF)
            keep_traces(0, s, h, jnp.dot(
                trace[gz, h], RAW[s, :, lanes].astype(BF16), preferred_element_type=F32
            ))

        @pl.when(s == 0)
        def _():
            peers = vert_total + (row > 0).astype(jnp.int32) + (row < last_row).astype(jnp.int32)
            pl.semaphore_wait(barrier, peers)

        @pl.when(s < 2)
        def _():
            send_halo(0, s)

        def split(r, carry):
            at = pl.ds(pl.multiple_of(r * 128, 128), 128)
            F[0, s, pl.ds(pl.multiple_of(NVT + r * 128, 8), 128), :] = RAW[s, :, at].T
            return carry

        lax.fori_loop(0, PLANE // 128, split, 0, unroll=18)
        return add(parts, plane_sums(0, s))

    send_sums(0, lax.fori_loop(0, 3, begin, nothing))
    send_halo(0, 2)

    for copy in consts[2:]:
        copy.wait()
    for s in range(3):
        z = speeds[s]
        up = jnp.where(gz == 0, axial[0], axial[1])
        down = jnp.where(gz == 0, axial[2], jnp.where(top_code == 2, axial[4], axial[3]))
        along = (z * jnp.where(z > 0, up, down)).astype(BF16)
        for h in range(2):
            W[s, h, 0:128, 128:256] = along[0:128]
            W[s, h, 128:256, 128:256] = jnp.zeros((128, 128), BF16)
            W[s, h, 128 + 32 * h : 160 + 32 * h, 128:256] = along[128:160]
        W[s, 0, :, 0:128] = radial[jnp.where(row == last_row, 1, 0)]
        W[s, 1, :, 0:128] = radial[2]

    inverse = 1.0 / ((row.astype(F32) + wall[2:3]) * ELEMENT_WIDTH)
    for k in range(3):
        TURN[k] = rows[2 + k] * inverse

    for n in range(STEPS):
        def move(s, none, n=n):
            ghosts(n, s)

            for h in range(2):
                x = F[n, s, NVT + h * HALF : NVT + (h + 1) * HALF, :].astype(BF16)
                operand = jnp.concatenate([x, G[s]], axis=1)
                TOUT[s, pl.ds(h * HALF, HALF), :] = jnp.dot(
                    operand, W[s, h], preferred_element_type=F32
                )

            def stream(a, carry):
                at = pl.ds(pl.multiple_of(a * NVT, 16), NVT)
                behind, ahead = (
                    F[n, s, pl.ds(pl.multiple_of((a + k) * NVT, 8), NVT), :] for k in (0, 2)
                )
                speed = (2 * a - (NVR - 1)).astype(F32) * UNIT
                base = (a + 1) * NVT
                around = (
                    TURN[1] * F[n, s, pl.ds(base + 1, NVT), :]
                    - TURN[2] * F[n, s, pl.ds(base - 1, NVT), :]
                )
                PART[s, at, :] = (
                    TURN[0] * (ahead - behind)
                    + speed * (around + TOUT[s, at, 0:128])
                    + TOUT[s, at, 128:256]
                )
                return carry

            lax.fori_loop(0, NVR, stream, 0, unroll=16)
            return none

        lax.fori_loop(0, 3, move, 0)
        params(wait_totals(n))

        def renew(s, parts, n=n):
            def update(a, carry):
                at = pl.ds(pl.multiple_of(a * NVT, 16), NVT)
                own = pl.ds(pl.multiple_of((a + 1) * NVT, 8), NVT)
                peak, heat, excess, wall_row = (BYR[s, k, pl.ds(a, 1), :] for k in range(4))
                goal = (BYT[0] * peak) * (1.0 + (BYT[1] + heat) * (BYT[2] + excess))
                F[(n + 1) % 2, s, own, :] = (
                    PR[0:1] * F[n, s, own, :] + PART[s, at, :] + wall_row * rows[1] + goal
                )
                return carry

            lax.fori_loop(0, NVR, update, 0, unroll=16)
            if n + 1 < STEPS:
                traces(n + 1, s)

                @pl.when(s < 2)
                def _():
                    send_halo(n + 1, s)

            return add(parts, plane_sums(n + 1, s))

        send_sums(n + 1, lax.fori_loop(0, 3, renew, nothing))
        if n + 1 < STEPS:
            send_halo(n + 1, 2)

    def back(r, carry):
        for s in range(3):
            x = F[STEPS % 2, s, pl.ds(pl.multiple_of(NVT + r * 128, 8), 128), :]
            out[:, pl.ds(pl.multiple_of(s * PLANE + r * 128, 128), 128)] = x.T
        return carry

    lax.fori_loop(0, PLANE // 128, back, 0, unroll=3)
    S = wait_totals(STEPS)
    density, u, temp, heat = observables(S)
    for i, value in enumerate([density] + u + [temp] + heat):
        PR[i : i + 1] = value
    final = PR[0:8]
    for r in range(8):
        macro[:, r, :] = final[:, r * 16 : (r + 1) * 16]
    flows = jnp.concatenate([S[3], S[4], jnp.zeros((6, 128), F32)], axis=0)
    edges = weight * jnp.dot(
        flows, edge[:, 256:384], preferred_element_type=F32, precision=lax.Precision.HIGHEST
    )
    incident, upward, downward = edges[1:2, 0:8], edges[0:1, 8:16], edges[1:2, 8:16]
    flux[...] = jnp.where(
        gz == 0,
        jnp.where(bottom_code == 1, SAT_DENSITY * half_flux - incident, 0.0),
        jnp.where(top_code == 2, upward - downward, 0.0),
    )

    for n in range(STEPS):
        for s in range(3):

            @pl.when(row > 0)
            def _():
                radial_copy(n, s, 0).wait_send()

            @pl.when(row < last_row)
            def _():
                radial_copy(n, s, 1).wait_send()

            axial_copy(n, s).wait_send()
    for n in range(STEPS + 1):
        each_peer(lambda peer, k, n=n: sum_copy(n, vert, peer, k).wait_send())


def deliver(new, macro, flux, new_hbm, macro_hbm, flux_hbm, sems):
    copies = [
        pltpu.make_async_copy(src, dst, sems.at[k])
        for k, (src, dst) in enumerate([(new, new_hbm), (macro, macro_hbm), (flux, flux_hbm)])
    ]
    for copy in copies:
        copy.start()
    for copy in copies:
        copy.wait()


def solution(mesh):
    row_total, vert_total = mesh.shape["row"], mesh.shape["vert"]
    arrays, weight, half_flux = constants()

    def on_device(distribution, z_order, edge_codes):
        f = distribution.reshape(128, 3 * PLANE)
        outs = (
            jax.ShapeDtypeStruct((128, 3 * PLANE), F32),
            jax.ShapeDtypeStruct((8, 8, 16), F32),
            jax.ShapeDtypeStruct((1, 8), F32),
        )
        hbm = pl.BlockSpec(memory_space=pl.ANY)
        smem = pl.BlockSpec(memory_space=pltpu.SMEM)
        vmem = pl.BlockSpec(memory_space=pltpu.VMEM)
        dma = pltpu.SemaphoreType.DMA
        new, macro, flux = pl.pallas_call(
            functools.partial(kernel, (row_total, vert_total), weight, half_flux),
            out_shape=(pltpu.VMEM(outs[0].shape, F32), outs[1], outs[2]),
            in_specs=[hbm, smem, smem] + [hbm] * len(arrays),
            out_specs=(vmem, vmem, vmem),
            scratch_shapes=[
                pltpu.VMEM((3, 128, PLANE), F32),
                pltpu.VMEM((2, 3, PLANE + 2 * NVT, 128), F32),
                pltpu.VMEM((3, HALF, 128), BF16),
                pltpu.VMEM((3, PLANE, 128), F32),
                pltpu.VMEM((3, PLANE, 256), F32),
                pltpu.VMEM((3, 2, 256, 256), BF16),
                pltpu.VMEM((3, NVT, 128), F32),
                pltpu.VMEM((3, NVT, 128), F32),
                pltpu.VMEM((3, 4, NVR, 128), F32),
                pltpu.VMEM((8, 128), F32),
            ]
            + [pltpu.VMEM(x.shape, x.dtype) for x in arrays]
            + [
                pltpu.VMEM((STEPS, 3, 2, 16, HALF), F32),
                pltpu.VMEM((STEPS, 3, 8, PLANE), F32),
                pltpu.VMEM((STEPS, 3, 2, 16, HALF), F32),
                pltpu.VMEM((STEPS, 3, 8, PLANE), F32),
                pltpu.VMEM((STEPS + 1, 16, 128), F32),
                pltpu.VMEM((STEPS + 1, vert_total, 16, 128), F32),
                dma((3,)),
                dma((len(arrays),)),
                dma((STEPS, 3, 2)),
                dma((STEPS, 3, 2)),
                dma((STEPS, 3)),
                dma((STEPS, 3)),
                dma((STEPS + 1, vert_total)),
                dma((STEPS + 1, vert_total)),
            ],
            compiler_params=pltpu.CompilerParams(
                collective_id=0, has_side_effects=True, vmem_limit_bytes=52 * 1024 * 1024
            ),
        )(f, z_order, edge_codes.reshape(2), *arrays)
        hold = lambda x: pltpu.with_memory_space_constraint(x, pltpu.VMEM)
        new, macro, flux = pl.pallas_call(
            deliver,
            out_shape=outs,
            in_specs=[vmem, vmem, vmem],
            out_specs=(hbm, hbm, hbm),
            scratch_shapes=[dma((3,))],
        )(hold(new), macro, flux)
        return new.reshape(distribution.shape), macro, flux

    in_specs = (P("row", "gz", "vert"), P("vert"), P(None, "row"))
    out_specs = (P("row", "gz", "vert"), P(None, "row", "gz"), P("gz", "row"))
    return jax.shard_map(
        on_device, mesh=mesh, in_specs=in_specs, out_specs=out_specs, check_vma=False
    )
```
